256 devices in a mesh: term: 32 (over z, x_lo, core), sector: 8 (over y, x_hi).
Axes of the slice: x: 4 (x_hi: 2, x_lo: 2; x = x_hi * 2 + x_lo), y: 4, z: 8, core: 2. Of those that a mesh axis runs over, the one named last changes fastest.
Arguments:
- wavefunction: bfloat16 [16, 512, 512], P('sector'), may hold values from -6 to 6
- left_operators: bfloat16 [2048, 512, 512], P(('term', 'sector')), may hold values from -0.25 to 0.25
- right_operators: bfloat16 [2048, 512, 512], P(('term', 'sector')), may hold values from -0.25 to 0.25
- source_sector: int32 [2048], P(('term', 'sector')), may hold values from 0 to 15
- target_sector: int32 [2048], P(('term', 'sector')), may hold values from 0 to 15
- live_terms: int32 [256], P(('term', 'sector')), may hold values from 1 to 8, as said below
- sector_rows: int32 [16], replicated, may hold values from 1 to 512, as said below
Outputs:
- sigma_blocks: float32 [16, 512, 512], P('sector', 'term')
The draws below stay inside these ranges and needn't reach their ends.
Inputs may be any that keep to these rules, and one draw needn't show every extreme that they name: Term group g = term index * 8 + sector index holds the term slots g * 8 to (g + 1) * 8 - 1; its live slots are the first live_terms[g]; some group has exactly 8. `sector_rows`: some sector uses exactly 512 rows.
All inputs are finite; a program needn't handle non-finite values.
Results may differ from the reference program's by a relative error of at most 0.0029.
Values may be sent and summed in bfloat16 or wider, within the bound.
No kernel may reach another device: no remote copies, remote signals or barrier semaphores. Data moves between devices by JAX's collectives and lax.ppermute only.
A program may use at most 128 MiB of HBM per device.

```python
import jax
import jax.numpy as jnp
from jax import lax

R = 512
C = 512
TERM_DEV = 8
NSEC = 16
TERMS = 2048
GROUPS = 256


def draw_live_terms(key, part):
    first = jax.random.fold_in(key, 11)
    second = jax.random.fold_in(key, 12)
    third = jax.random.fold_in(key, 13)
    small = jax.random.randint(first, (GROUPS,), 1, 3)
    heavy = jax.random.randint(second, (GROUPS,), 0, 16) == 0
    chosen = jax.random.randint(third, (), 0, GROUPS)
    heavy = heavy | (jnp.arange(GROUPS, dtype=jnp.int32) == chosen)
    return jnp.where(heavy, TERM_DEV, small).astype(jnp.int32)


def draw_sector_rows(key, part):
    first = jax.random.fold_in(key, 21)
    second = jax.random.fold_in(key, 22)
    third = jax.random.fold_in(key, 23)
    fourth = jax.random.fold_in(key, 24)
    fifth = jax.random.fold_in(key, 25)
    sizes_one = jax.random.randint(first, (NSEC,), 1, R + 1)
    sizes_two = jax.random.randint(second, (NSEC,), 1, R + 1)
    sizes = jnp.minimum(sizes_one, sizes_two)
    chosen = jax.random.randint(third, (), 0, NSEC)
    offset = jax.random.randint(fourth, (), 1, NSEC)
    partner = (chosen + offset) % NSEC
    partner_rows = jax.random.randint(fifth, (), R // 2, R)
    sector_ids = jnp.arange(NSEC, dtype=jnp.int32)
    sizes = jnp.where(sector_ids == partner, partner_rows, sizes)
    sizes = jnp.where(sector_ids == chosen, R, sizes)
    return sizes.astype(jnp.int32)


def set_ends(values, stream_key, smallest, high):
    longest = values.shape.index(max(values.shape))
    spots = []
    for shift in (0, 1):
        where = [jax.random.randint(jax.random.fold_in(stream_key, axis), (), 0, length) for axis, length in enumerate(values.shape)]
        where[longest] = (where[longest] + shift) % values.shape[longest]
        spots.append(tuple(where))
    return values.at[spots[0]].set(smallest).at[spots[1]].set(high)


def block_levels(stream_key, dims, pieces, low, largest):
    factor_of, own = 1.0, jax.random.fold_in(stream_key, 6)
    for position, blocks in pieces:
        steps = jnp.exp(jax.random.uniform(jax.random.fold_in(own, position), (blocks,), jnp.float32, low / len(pieces), largest / len(pieces)))
        factor_of = factor_of * jnp.repeat(steps, dims[position] // blocks).reshape([-1 if axis == position else 1 for axis in range(len(dims))])
    return factor_of


def normal_values(own_key, extent, deviation, reach, pieces=(), kind=jnp.bfloat16):
    result = jax.random.normal(own_key, extent, jnp.float32) * deviation
    if len(pieces) > 0:
        result = block_levels(own_key, extent, pieces, -0.22, 0.18) * result
    return jnp.clip(result, min=-reach, max=reach).astype(kind)


def setup_inputs(seed: int = 0) -> dict:
    key_of = jax.random.split(jax.random.key(seed), 8)
    wavefunction = normal_values(key_of[0], (NSEC, R, C), 1.0, 6.0, ((0, 8),))
    left_operators = normal_values(key_of[1], (TERMS, R, R), R ** -0.5, 0.25, ((0, 256),))
    right_operators = normal_values(key_of[2], (TERMS, C, C), C ** -0.5, 0.25, ((0, 256),))
    source_sector = set_ends(jax.random.randint(key_of[3], (TERMS,), 0, NSEC), jax.random.fold_in(key_of[3], 1), 0, NSEC - 1).astype(jnp.int32)
    target_sector = set_ends(jax.random.randint(key_of[4], (TERMS,), 0, NSEC), jax.random.fold_in(key_of[4], 1), 0, NSEC - 1).astype(jnp.int32)
    live_terms = draw_live_terms(jax.random.fold_in(key_of[7], 71), 0)
    sector_rows = draw_sector_rows(jax.random.fold_in(key_of[7], 71), 0)
    return dict(wavefunction=wavefunction, left_operators=left_operators, right_operators=right_operators, source_sector=source_sector, target_sector=target_sector, live_terms=live_terms, sector_rows=sector_rows)


def reference(wavefunction, left_operators, right_operators, source_sector, target_sector, live_terms, sector_rows):
    row_ids = jnp.arange(R, dtype=jnp.int32)
    slot_ids = jnp.arange(TERMS, dtype=jnp.int32)
    live_mask = (slot_ids % TERM_DEV) < live_terms[slot_ids // TERM_DEV]
    sigma = jnp.zeros((NSEC, R, C), jnp.float32)

    def apply_term(slot, partial_value):
        def contribute(partial_value):
            source_index = source_sector[slot].astype(jnp.int32)
            target_index = target_sector[slot].astype(jnp.int32)
            source = lax.dynamic_index_in_dim(wavefunction, source_index, 0, keepdims=False)
            keep_rows = (row_ids < sector_rows[source_index])[:, None]
            source = jnp.where(keep_rows, source, jnp.zeros_like(source))
            left_half = jnp.dot(left_operators[slot], source, preferred_element_type=jnp.float32).astype(jnp.bfloat16)
            product = lax.dot_general(left_half, right_operators[slot], (((1,), (1,)), ((), ())), preferred_element_type=jnp.float32)
            current = lax.dynamic_index_in_dim(partial_value, target_index, 0, keepdims=True)
            return lax.dynamic_update_index_in_dim(partial_value, current + product[None], target_index, 0)

        return lax.cond(live_mask[slot], contribute, lambda kept: kept, partial_value)

    sigma = lax.fori_loop(0, TERMS, apply_term, sigma)
    used = row_ids[None, :, None] < sector_rows[:, None, None]
    return jnp.where(used, sigma, jnp.zeros_like(sigma))
```

```python
import functools

import jax
import jax.numpy as jnp
from jax import lax
from jax.experimental import pallas as pl
from jax.experimental.pallas import tpu as pltpu
from jax.sharding import PartitionSpec as P

UNIT = 32
AXES = ("term", "sector")
DEPTH = 3


def device_index(x, y, z, core):
    x, y, z = x % 4, y % 4, z % 8
    return (z * 4 + (x % 2) * 2 + core) * 8 + y * 2 + x // 2


def pairs(move):
    every = [(x, y, z, c) for x in range(4) for y in range(4) for z in range(8) for c in range(2)]
    return [(device_index(*at), device_index(*move(*at))) for at in every]


OTHER_CORE = pairs(lambda x, y, z, c: (x, y, z, 1 - c))
FIRST_AXIS = [pairs(lambda x, y, z, c: (x + k * c, y + k * (1 - c), z, c)) for k in range(4)]
SECOND_AXIS = [pairs(lambda x, y, z, c: (x + k * (1 - c), y + k * c, z, c)) for k in range(4)]


def coordinates():
    term, sector = lax.axis_index("term"), lax.axis_index("sector")
    x_lo, core = lax.rem(lax.div(term, 2), 2), lax.rem(term, 2)
    return 2 * lax.rem(sector, 2) + x_lo, lax.div(sector, 2), lax.div(term, 4), core


def units_of(rows):
    return lax.div(rows + (UNIT - 1), UNIT)


def group_entry(core, place, i):
    along_x = 4 * lax.div(i, 2) + 2 * lax.div(place, 2) + lax.rem(i, 2)
    sector = jnp.where(core == 0, 4 * place + lax.rem(i, 4), along_x)
    first = jnp.where(core == 0, 0, lax.rem(place, 2))
    return sector, first, 1 + core


def group_count(rows_ref, core, place, i):
    sector, first, step = group_entry(core, place, i)
    count = lax.div(units_of(rows_ref[sector]) - first + step - 1, step)
    return jnp.where((core == 0) & (i >= 4), 0, jnp.maximum(count, 0))


def pack_kernel(rows_ref, wave_ref, out_ref, packed, sems):
    core = lax.rem(lax.axis_index("term"), 2)
    sector = lax.axis_index("sector")
    first_units = units_of(rows_ref[2 * sector])
    second_units = units_of(rows_ref[2 * sector + 1])

    def copy_half(half):
        lanes = pl.ds(half * 256, 256)
        for b, units, base in ((0, first_units, 0), (1, second_units, first_units)):

            @pl.loop(0, units)
            def _(u):
                at = pl.multiple_of((base + u) * UNIT, UNIT)
                packed[pl.ds(at, UNIT), :] = wave_ref[b, pl.ds(pl.multiple_of(u * UNIT, UNIT), UNIT), lanes]

    for half in range(2):
        pl.when(core == half)(functools.partial(copy_half, half))
    copies = [pltpu.make_async_copy(packed, out_ref.at[j], sems.at[j]) for j in range(out_ref.shape[0])]
    for copy in copies:
        copy.start()
    for copy in copies:
        copy.wait()


def pack_wave(sector_rows, wavefunction, rows):
    return pl.pallas_call(
        pack_kernel,
        out_shape=jax.ShapeDtypeStruct((8, rows, 256), jnp.bfloat16),
        in_specs=[pl.BlockSpec(memory_space=pltpu.SMEM), pl.BlockSpec(memory_space=pltpu.VMEM)],
        out_specs=pl.BlockSpec(memory_space=pl.ANY),
        scratch_shapes=[pltpu.VMEM((rows, 256), jnp.bfloat16), pltpu.SemaphoreType.DMA((8,))],
        compiler_params=pltpu.CompilerParams(vmem_limit_bytes=24 * 1024 * 1024),
        name="pack_wave",
    )(sector_rows, wavefunction)


def terms_kernel(
    wave_rows,
    rows_ref,
    source_ref,
    target_ref,
    live_ref,
    far_ref,
    near_wave,
    far_wave,
    near_left,
    near_right,
    far_left,
    far_right,
    own_ref,
    send1,
    send2,
    send3,
    acc,
    left_buf,
    right_buf,
    wave_buf,
    half_buf,
    sems,
):
    x, y, _, core = coordinates()
    near_live = live_ref[0]
    total = near_live + far_ref[16]
    last_start = 8 * wave_rows - 512

    def facts(i):
        near = i < near_live
        slot = jnp.where(near, i, i - near_live)
        source = jnp.where(near, source_ref[slot], far_ref[slot])
        target = jnp.where(near, target_ref[slot], far_ref[8 + slot])
        return near, slot, source, target

    def wave_place(source):
        pair = lax.div(source, 2)
        before = jnp.where(lax.rem(source, 2) == 1, units_of(rows_ref[2 * pair]), 0) * UNIT
        want = pair * wave_rows + before
        start = jnp.minimum(want, last_start)
        return pl.multiple_of(start, UNIT), pl.multiple_of(want - start, UNIT)

    def copies(near, slot, source, buf):
        start, _ = wave_place(source)
        left = near_left if near else far_left
        right = near_right if near else far_right
        lanes = pl.ds(pl.multiple_of(core * 256, 256), 256)
        return (
            pltpu.make_async_copy(left.at[slot], left_buf.at[buf], sems.at[buf, 0]),
            pltpu.make_async_copy(right.at[slot, lanes], right_buf.at[buf], sems.at[buf, 1]),
            pltpu.make_async_copy(
                near_wave.at[pl.ds(start, 512)], wave_buf.at[buf, 0, pl.ds(0, 512)], sems.at[buf, 2]
            ),
            pltpu.make_async_copy(
                far_wave.at[pl.ds(start, 512)], wave_buf.at[buf, 1, pl.ds(0, 512)], sems.at[buf, 3]
            ),
        )

    def begin(i):
        near, slot, source, _ = facts(i)
        buf = lax.rem(i, DEPTH)

        @pl.when(near)
        def _():
            for copy in copies(True, slot, source, buf):
                copy.start()

        @pl.when(jnp.logical_not(near))
        def _():
            for copy in copies(False, slot, source, buf):
                copy.start()

    for i in range(DEPTH - 1):
        pl.when(i < total)(functools.partial(begin, i))

    for q in range(16):

        @pl.loop(0, units_of(rows_ref[q]))
        def _(u):
            acc[pl.ds(pl.multiple_of(q * 512 + u * UNIT, UNIT), UNIT), :] = jnp.zeros((UNIT, 256), jnp.float32)

    @pl.loop(0, total)
    def _(i):
        pl.when(i + DEPTH - 1 < total)(lambda: begin(i + DEPTH - 1))
        near, slot, source, target = facts(i)
        buf = lax.rem(i, DEPTH)
        for copy in copies(True, slot, source, buf):
            copy.wait()
        _, shift = wave_place(source)
        source_rows = rows_ref[source]
        target_rows = rows_ref[target]

        def product(row, depth):
            keep = lax.broadcasted_iota(jnp.int32, (depth, 1), 0) < source_rows
            left = left_buf[buf, pl.ds(row, 256), pl.ds(0, depth)]
            for wave_half in range(2):
                wave = wave_buf[buf, wave_half, pl.ds(shift, depth), :]
                wave = jnp.where(keep, wave, jnp.zeros_like(wave))
                half = jnp.dot(left, wave, preferred_element_type=jnp.float32)
                half_buf[wave_half] = half.astype(jnp.bfloat16)
            for low in range(2):

                @pl.when(core == low)
                def _():
                    halves = (half_buf[low], half_buf[1 - low])
                    both = jnp.concatenate(halves, axis=1)
                    out = lax.dot_general(
                        both, right_buf[buf], (((1,), (1,)), ((), ())), preferred_element_type=jnp.float32
                    )
                    at = pl.ds(pl.multiple_of(target * 512 + row, 256), 256)
                    acc[at, :] += out

        for row in range(0, 512, 256):
            pl.when((target_rows > row) & (source_rows <= 256))(functools.partial(product, row, 256))
            pl.when((target_rows > row) & (source_rows > 256))(functools.partial(product, row, 512))

    place = jnp.where(core == 0, y, x)
    for k, dest in enumerate((own_ref, send1, send2, send3)):
        there = lax.rem(place + k, 4)

        def one_sector(i, filled):
            sector, first, step = group_entry(core, there, i)
            count = group_count(rows_ref, core, there, i)

            @pl.loop(0, count)
            def _(j):
                at = pl.multiple_of(sector * 512 + (first + step * j) * UNIT, UNIT)
                to = pl.multiple_of((filled + j) * UNIT, UNIT)
                dest[pl.ds(to, UNIT), :] = acc[pl.ds(at, UNIT), :].astype(dest.dtype)

            return filled + count

        lax.fori_loop(0, 8, one_sector, 0)


def term_products(rows, small, far_small, near_wave, far_wave, near_left, near_right, far_left, far_right, group_rows):
    wave_rows = near_wave.shape[0] // 8
    smem = pl.BlockSpec(memory_space=pltpu.SMEM)
    hbm = pl.BlockSpec(memory_space=pl.ANY)
    vmem = pl.BlockSpec(memory_space=pltpu.VMEM)
    send = jax.ShapeDtypeStruct((group_rows, 256), jnp.bfloat16)
    return pl.pallas_call(
        functools.partial(terms_kernel, wave_rows),
        out_shape=(jax.ShapeDtypeStruct((group_rows, 256), jnp.float32), send, send, send),
        in_specs=[smem] * 5 + [hbm] * 6,
        out_specs=(vmem,) * 4,
        scratch_shapes=[
            pltpu.VMEM((16 * 512, 256), jnp.float32),
            pltpu.VMEM((DEPTH, 512, 512), jnp.bfloat16),
            pltpu.VMEM((DEPTH, 256, 512), jnp.bfloat16),
            pltpu.VMEM((DEPTH, 2, 1024, 256), jnp.bfloat16),
            pltpu.VMEM((2, 256, 256), jnp.bfloat16),
            pltpu.SemaphoreType.DMA((DEPTH, 4)),
        ],
        compiler_params=pltpu.CompilerParams(vmem_limit_bytes=48 * 1024 * 1024),
        cost_estimate=pl.CostEstimate(flops=8 * 10**9, bytes_accessed=16 * 2**20, transcendentals=0),
        name="term_products",
    )(rows, *small, far_small, near_wave, far_wave, near_left, near_right, far_left, far_right)


def regroup_kernel(rows_ref, own_ref, got1, got2, got3, keep_ref, send1, send2, send3, blocks):
    x, y, _, core = coordinates()
    place, other = jnp.where(core == 0, y, x), jnp.where(core == 0, x, y)
    blocks[...] = jnp.zeros_like(blocks)

    def one_sector(i, filled):
        _, first, step = group_entry(core, place, i)
        count = group_count(rows_ref, core, place, i)

        @pl.loop(0, count)
        def _(j):
            unit = first + step * j
            at = pl.ds(pl.multiple_of((filled + j) * UNIT, UNIT), UNIT)
            total = own_ref[at, :] + got1[at, :].astype(jnp.float32)
            total = total + got2[at, :].astype(jnp.float32)
            total = total + got3[at, :].astype(jnp.float32)
            there = jnp.where(core == 0, 2 * lax.div(i, 2) + lax.rem(unit, 2), lax.div(i, 2))
            k = lax.rem(there - other + 4, 4)
            to = pl.multiple_of((lax.rem(i, 2) * 8 + lax.div(unit, 2)) * UNIT, UNIT)
            blocks[k, pl.ds(to, UNIT), :] = total

        return filled + count

    lax.fori_loop(0, 8, one_sector, 0)
    keep_ref[...] = blocks[0]
    for k, dest in enumerate((send1, send2, send3)):
        dest[...] = blocks[k + 1].astype(jnp.bfloat16)


def regroup(rows, own, got):
    vmem = pl.BlockSpec(memory_space=pltpu.VMEM)
    send = jax.ShapeDtypeStruct((512, 256), jnp.bfloat16)
    return pl.pallas_call(
        regroup_kernel,
        out_shape=(jax.ShapeDtypeStruct((512, 256), jnp.float32), send, send, send),
        in_specs=[pl.BlockSpec(memory_space=pltpu.SMEM)] + [vmem] * 4,
        out_specs=(vmem,) * 4,
        scratch_shapes=[pltpu.VMEM((4, 512, 256), jnp.float32)],
        compiler_params=pltpu.CompilerParams(vmem_limit_bytes=32 * 1024 * 1024),
        name="regroup",
    )(rows, own, *got)


def spread_kernel(keep_ref, got1, got2, got3, out_ref):
    total = keep_ref[...] + got1[...].astype(jnp.float32)
    total = total + got2[...].astype(jnp.float32)
    total = (total + got3[...].astype(jnp.float32)).astype(jnp.bfloat16)
    for b in range(2):
        for z in range(8):
            for core in range(2):
                start = (b * 8 + z) * UNIT + core * 16
                out_ref[z * 2 + core, b] = total[start : start + 16]


def spread(keep, got):
    vmem = pl.BlockSpec(memory_space=pltpu.VMEM)
    return pl.pallas_call(
        spread_kernel,
        out_shape=jax.ShapeDtypeStruct((16, 2, 16, 256), jnp.bfloat16),
        in_specs=[vmem] * 4,
        out_specs=vmem,
        name="spread",
    )(keep, *got)


def finish_kernel(rows_ref, parts_ref, out_ref):
    term, sector = lax.axis_index("term"), lax.axis_index("sector")
    row = term * 16 + lax.broadcasted_iota(jnp.int32, (16, 1), 0)
    for b in range(2):
        used = row < rows_ref[2 * sector + b]
        for half in range(2):
            total = parts_ref[half, b].astype(jnp.float32)
            for z in range(1, 8):
                total = total + parts_ref[z * 2 + half, b].astype(jnp.float32)
            out_ref[b, :, half * 256 : half * 256 + 256] = jnp.where(used, total, jnp.zeros_like(total))


def finish(rows, parts):
    vmem = pl.BlockSpec(memory_space=pltpu.VMEM)
    return pl.pallas_call(
        finish_kernel,
        out_shape=jax.ShapeDtypeStruct((2, 16, 512), jnp.float32),
        in_specs=[pl.BlockSpec(memory_space=pltpu.SMEM), vmem],
        out_specs=vmem,
        name="finish",
    )(rows, parts)


def local(
    wavefunction,
    left_operators,
    right_operators,
    source_sector,
    target_sector,
    live_terms,
    sector_rows,
    wave_rows=1024,
    group_rows=2048,
):
    swap = functools.partial(lax.ppermute, axis_name=AXES, perm=OTHER_CORE)
    far_small = swap(jnp.concatenate([source_sector, target_sector, live_terms]))
    far_left, far_right = swap(left_operators), swap(right_operators)
    packed = pack_wave(sector_rows, wavefunction, wave_rows)
    near_wave = lax.all_to_all(packed, "sector", split_axis=0, concat_axis=0, tiled=True)
    far_wave = swap(near_wave)
    small = (source_sector, target_sector, live_terms)
    own, *sends = term_products(
        sector_rows,
        small,
        far_small,
        near_wave.reshape(-1, 256),
        far_wave.reshape(-1, 256),
        left_operators,
        right_operators,
        far_left,
        far_right,
        group_rows,
    )
    got = [lax.ppermute(s, AXES, FIRST_AXIS[k + 1]) for k, s in enumerate(sends)]
    keep, *sends = regroup(sector_rows, own, got)
    got = [lax.ppermute(s, AXES, SECOND_AXIS[k + 1]) for k, s in enumerate(sends)]
    parts = spread(keep, got)
    groups = [[z * 4 + x_lo * 2 + core for z in range(8) for core in range(2)] for x_lo in range(2)]
    arrived = lax.all_to_all(
        parts, "term", split_axis=0, concat_axis=0, axis_index_groups=groups, tiled=True
    )
    return finish(sector_rows, arrived)


def solution(mesh):
    in_specs = (
        P("sector", None, None),
        P(("term", "sector"), None, None),
        P(("term", "sector"), None, None),
        P(("term", "sector")),
        P(("term", "sector")),
        P(("term", "sector")),
        P(),
    )
    out_specs = P("sector", "term", None)
    return jax.shard_map(local, mesh=mesh, in_specs=in_specs, out_specs=out_specs, check_vma=False)
```

```python
import functools

import jax
import jax.numpy as jnp
from jax import lax
from jax.experimental import pallas as pl
from jax.experimental.pallas import tpu as pltpu
from jax.sharding import PartitionSpec as P

UNIT = 32
AXES = ("term", "sector")
DEPTH = 3
SIZES = ((24, 34), (28, 38), (28, 44), (32, 64))


def device_index(x, y, z, core):
    x, y, z = x % 4, y % 4, z % 8
    return (z * 4 + (x % 2) * 2 + core) * 8 + y * 2 + x // 2


def pairs(move):
    every = [(x, y, z, c) for x in range(4) for y in range(4) for z in range(8) for c in range(2)]
    return [(device_index(*at), device_index(*move(*at))) for at in every if move(*at) is not None]


OTHER_CORE = pairs(lambda x, y, z, c: (x, y, z, 1 - c))
FIRST_AXIS = [pairs(lambda x, y, z, c: (x + k * c, y + k * (1 - c), z, c)) for k in range(4)]
ACROSS = (3, 2, 1, 0)
GATHER_FIRST = [
    pairs(lambda x, y, z, c: (x, y + 1, z, c) if c else (ACROSS[x], y, z, c)),
    pairs(lambda x, y, z, c: (x, y + 2, z, c) if c else None),
    pairs(lambda x, y, z, c: (x, y + 3, z, c) if c else None),
]
GATHER_SECOND = [
    pairs(lambda x, y, z, c: (ACROSS[x], y, z, c) if c else (x, y + 1, z, c)),
    pairs(lambda x, y, z, c: (ACROSS[x], y, z, c) if c else (x, y + 2, z, c)),
    pairs(lambda x, y, z, c: None if c else (x, y + 3, z, c)),
]
FROM_CORE_0 = pairs(lambda x, y, z, c: None if c else (x, y, z, 1))
SECOND_AXIS = [pairs(lambda x, y, z, c: (x + k * (1 - c), y + k * c, z, c)) for k in range(4)]


def coordinates():
    term, sector = lax.axis_index("term"), lax.axis_index("sector")
    x_lo, core = lax.rem(lax.div(term, 2), 2), lax.rem(term, 2)
    return 2 * lax.rem(sector, 2) + x_lo, lax.div(sector, 2), lax.div(term, 4), core


def units_of(rows):
    return lax.div(rows + (UNIT - 1), UNIT)


def group_entry(core, place, i):
    along_x = 4 * lax.div(i, 2) + 2 * lax.div(place, 2) + lax.rem(i, 2)
    sector = jnp.where(core == 0, 4 * place + lax.rem(i, 4), along_x)
    first = jnp.where(core == 0, 0, lax.rem(place, 2))
    return sector, first, 1 + core


def group_count(rows_ref, core, place, i):
    sector, first, step = group_entry(core, place, i)
    count = lax.div(units_of(rows_ref[sector]) - first + step - 1, step)
    return jnp.where((core == 0) & (i >= 4), 0, jnp.maximum(count, 0))


def unit_at(u):
    return pl.ds(pl.multiple_of(u * UNIT, UNIT), UNIT)


def choose_kernel(sizes, rows_ref, out_ref):
    units = [units_of(rows_ref[q]) for q in range(16)]
    pair = functools.reduce(jnp.maximum, [units[q] + units[q + 1] for q in range(0, 16, 2)])
    along_y = functools.reduce(jnp.maximum, [sum(units[q : q + 4]) for q in range(0, 16, 4)])
    along_x, across = jnp.int32(0), jnp.int32(0)
    for x_hi in range(2):
        mine = [units[q] for q in range(16) if (q // 2) % 2 == x_hi]
        across = jnp.maximum(across, sum(mine))
        along_x = jnp.maximum(along_x, sum(lax.div(n + 1, 2) for n in mine))
    group = jnp.maximum(jnp.maximum(along_y, along_x), lax.div(across + 1, 2))
    chosen = jnp.int32(len(sizes) - 1)
    for i in reversed(range(len(sizes) - 1)):
        chosen = jnp.where((pair <= sizes[i][0]) & (group <= sizes[i][1]), i, chosen)
    out_ref[0] = chosen


def choose(sector_rows, sizes):
    smem = pl.BlockSpec(memory_space=pltpu.SMEM)
    return pl.pallas_call(
        functools.partial(choose_kernel, sizes),
        out_shape=jax.ShapeDtypeStruct((1,), jnp.int32),
        in_specs=[smem],
        out_specs=smem,
        name="choose",
    )(sector_rows)[0]


def pack_kernel(rows_ref, wave_ref, out_ref):
    core = lax.rem(lax.axis_index("term"), 2)
    sector = lax.axis_index("sector")
    first_units = units_of(rows_ref[2 * sector])
    second_units = units_of(rows_ref[2 * sector + 1])

    def copy_half(half):
        lanes = pl.ds(half * 256, 256)
        for b, units, base in ((0, first_units, 0), (1, second_units, first_units)):

            @pl.loop(0, units)
            def _(u):
                out_ref[unit_at(base + u), :] = wave_ref[b, unit_at(u), lanes]

    for half in range(2):
        pl.when(core == half)(functools.partial(copy_half, half))


def pack_wave(sector_rows, wavefunction, rows):
    vmem = pl.BlockSpec(memory_space=pltpu.VMEM)
    return pl.pallas_call(
        pack_kernel,
        out_shape=jax.ShapeDtypeStruct((rows, 256), jnp.bfloat16),
        in_specs=[pl.BlockSpec(memory_space=pltpu.SMEM), vmem],
        out_specs=vmem,
        compiler_params=pltpu.CompilerParams(vmem_limit_bytes=16 * 1024 * 1024),
        name="pack_wave",
    )(sector_rows, wavefunction)


def join_kernel(rows_ref, own_ref, got1, got2, got3, both_ref, send2_ref, send1_ref):
    x, y, _, core = coordinates()
    x_hi = lax.div(x, 2)
    block_rows = send1_ref.shape[0]

    def one_pair(p, filled):
        pair = jnp.where(core == 0, 2 * y + p, 2 * p + x_hi)
        count = units_of(rows_ref[2 * pair]) + units_of(rows_ref[2 * pair + 1])
        count = jnp.where((core == 0) & (p >= 2), 0, count)
        from_x = jnp.where(p == x_hi, 0, 1)
        k = jnp.where(core == 0, from_x, lax.rem(y - p + 4, 4))
        for source, block in enumerate((own_ref, got1, got2, got3)):

            @pl.loop(0, jnp.where(k == source, count, 0))
            def _(u):
                both_ref[unit_at(filled + u), :] = block[unit_at(u), :]

        return filled + count

    lax.fori_loop(0, 4, one_pair, 0)
    send1_ref[...] = both_ref[:block_rows]

    @pl.when(core == 0)
    def _():
        send2_ref[...] = both_ref[:block_rows]

    @pl.when(core == 1)
    def _():
        send2_ref[...] = both_ref[block_rows:]


def join(sector_rows, own, got, rows):
    vmem = pl.BlockSpec(memory_space=pltpu.VMEM)
    block = jax.ShapeDtypeStruct((rows, 256), jnp.bfloat16)
    return pl.pallas_call(
        join_kernel,
        out_shape=(jax.ShapeDtypeStruct((2 * rows, 256), jnp.bfloat16), block, block),
        in_specs=[pl.BlockSpec(memory_space=pltpu.SMEM)] + [vmem] * 4,
        out_specs=(vmem,) * 3,
        compiler_params=pltpu.CompilerParams(vmem_limit_bytes=24 * 1024 * 1024),
        name="join",
    )(sector_rows, own, *got)


def terms_kernel(
    block_units,
    rows_ref,
    source_ref,
    target_ref,
    live_ref,
    far_ref,
    near0,
    near1,
    near2,
    near3,
    far0,
    far1,
    far2,
    far3,
    near_left,
    near_right,
    far_left,
    far_right,
    own_ref,
    send1,
    send2,
    send3,
    acc,
    left_buf,
    right_buf,
    wave_buf,
    half_buf,
    sems,
):
    x, y, _, core = coordinates()
    near_live = live_ref[0]
    total = near_live + far_ref[16]

    def facts(i):
        near = i < near_live
        slot = jnp.where(near, i, i - near_live)
        source = jnp.where(near, source_ref[slot], far_ref[slot])
        target = jnp.where(near, target_ref[slot], far_ref[8 + slot])
        return near, slot, source, target

    def copies(near, slot, buf):
        left = near_left if near else far_left
        right = near_right if near else far_right
        lanes = pl.ds(pl.multiple_of(core * 256, 256), 256)
        return (
            pltpu.make_async_copy(left.at[slot], left_buf.at[buf], sems.at[buf, 0]),
            pltpu.make_async_copy(right.at[slot, lanes], right_buf.at[buf], sems.at[buf, 1]),
        )

    def begin(i):
        near, slot, _, _ = facts(i)
        buf = lax.rem(i, DEPTH)

        @pl.when(near)
        def _():
            for copy in copies(True, slot, buf):
                copy.start()

        @pl.when(jnp.logical_not(near))
        def _():
            for copy in copies(False, slot, buf):
                copy.start()

    for i in range(DEPTH - 1):
        pl.when(i < total)(functools.partial(begin, i))

    for q in range(16):

        @pl.loop(0, units_of(rows_ref[q]))
        def _(u):
            acc[unit_at(q * 16 + u), :] = jnp.zeros((UNIT, 256), jnp.float32)

    def fetch(source, units):
        source_y = lax.div(source, 4)
        pair = lax.div(source, 2)
        odd = lax.rem(source, 2)
        before_odd = jnp.where(odd == 1, units_of(rows_ref[2 * pair]), 0)
        k = lax.rem(y - source_y + 4, 4)
        before = jnp.where(
            lax.rem(pair, 2) == 1, units_of(rows_ref[4 * source_y]) + units_of(rows_ref[4 * source_y + 1]), 0
        )
        in_y = jnp.where(k == 0, 0, k + 1) * block_units + before + before_odd
        source_hi = lax.rem(pair, 2)
        before = before_odd
        for p in range(3):
            both = units_of(rows_ref[4 * p + 2 * source_hi]) + units_of(rows_ref[4 * p + 2 * source_hi + 1])
            before = before + jnp.where(p < source_y, both, 0)
        in_x = jnp.where(source_hi == lax.div(x, 2), 0, 2) * block_units + before
        for memory, layout, half in (
            ((near0, near1, near2, near3), core, core),
            ((far0, far1, far2, far3), 1 - core, 1 - core),
        ):
            first = jnp.where(layout == 0, in_y, in_x)
            low = 0
            for block in memory:
                high = low + block.shape[0] // UNIT
                begin_at, end_at = jnp.maximum(first, low), jnp.minimum(first + units, high)

                @pl.loop(begin_at, end_at)
                def _(u):
                    wave_buf[half, unit_at(u - first), :] = block[unit_at(u - low), :]

                low = high

    @pl.loop(0, total)
    def _(i):
        pl.when(i + DEPTH - 1 < total)(lambda: begin(i + DEPTH - 1))
        near, slot, source, target = facts(i)
        buf = lax.rem(i, DEPTH)
        source_rows = rows_ref[source]
        target_rows = rows_ref[target]
        fetch(source, units_of(source_rows))
        for copy in copies(True, slot, buf):
            copy.wait()

        def product(height, depth):
            keep = lax.broadcasted_iota(jnp.int32, (depth, 1), 0) < source_rows
            left = left_buf[buf, pl.ds(0, height), pl.ds(0, depth)]
            for half in range(2):
                wave = wave_buf[half, pl.ds(0, depth), :]
                wave = jnp.where(keep, wave, jnp.zeros_like(wave))
                part = jnp.dot(left, wave, preferred_element_type=jnp.float32)
                half_buf[pl.ds(0, height), half * 256 : half * 256 + 256] = part.astype(jnp.bfloat16)
            out = lax.dot_general(
                half_buf[pl.ds(0, height), :],
                right_buf[buf],
                (((1,), (1,)), ((), ())),
                preferred_element_type=jnp.float32,
            )
            acc[pl.ds(pl.multiple_of(target * 512, 512), height), :] += out

        for height in (256, 512):
            for depth in (256, 512):
                low_rows = (target_rows > 256) if height == 512 else (target_rows <= 256)
                low_depth = (source_rows > 256) if depth == 512 else (source_rows <= 256)
                pl.when(low_rows & low_depth)(functools.partial(product, height, depth))

    place = jnp.where(core == 0, y, x)
    for k, dest in enumerate((own_ref, send1, send2, send3)):
        there = lax.rem(place + k, 4)

        def one_sector(i, filled):
            sector, first, step = group_entry(core, there, i)
            count = group_count(rows_ref, core, there, i)

            @pl.loop(0, count)
            def _(j):
                tile = acc[unit_at(sector * 16 + first + step * j), :]
                dest[unit_at(filled + j), :] = tile.astype(dest.dtype)

            return filled + count

        lax.fori_loop(0, 8, one_sector, 0)


def term_products(rows, small, far_small, near, far, operators, group_rows):
    smem = pl.BlockSpec(memory_space=pltpu.SMEM)
    hbm = pl.BlockSpec(memory_space=pl.ANY)
    vmem = pl.BlockSpec(memory_space=pltpu.VMEM)
    send = jax.ShapeDtypeStruct((group_rows, 256), jnp.bfloat16)
    return pl.pallas_call(
        functools.partial(terms_kernel, group_rows // UNIT),
        out_shape=(jax.ShapeDtypeStruct((group_rows, 256), jnp.float32), send, send, send),
        in_specs=[smem] * 5 + [vmem] * 8 + [hbm] * 4,
        out_specs=(vmem,) * 4,
        scratch_shapes=[
            pltpu.VMEM((16 * 512, 256), jnp.float32),
            pltpu.VMEM((DEPTH, 512, 512), jnp.bfloat16),
            pltpu.VMEM((DEPTH, 256, 512), jnp.bfloat16),
            pltpu.VMEM((2, 512, 256), jnp.bfloat16),
            pltpu.VMEM((512, 512), jnp.bfloat16),
            pltpu.SemaphoreType.DMA((DEPTH, 2)),
        ],
        compiler_params=pltpu.CompilerParams(vmem_limit_bytes=48 * 1024 * 1024),
        cost_estimate=pl.CostEstimate(flops=8 * 10**9, bytes_accessed=16 * 2**20, transcendentals=0),
        name="term_products",
    )(rows, *small, far_small, *near, *far, *operators)


def regroup_kernel(rows_ref, own_ref, got1, got2, got3, keep_ref, send1, send2, send3, blocks):
    x, y, _, core = coordinates()
    place, other = jnp.where(core == 0, y, x), jnp.where(core == 0, x, y)
    blocks[...] = jnp.zeros_like(blocks)

    def one_sector(i, filled):
        _, first, step = group_entry(core, place, i)
        count = group_count(rows_ref, core, place, i)

        @pl.loop(0, count)
        def _(j):
            unit = first + step * j
            at = pl.ds(pl.multiple_of((filled + j) * UNIT, UNIT), UNIT)
            total = own_ref[at, :] + got1[at, :].astype(jnp.float32)
            total = total + got2[at, :].astype(jnp.float32)
            total = total + got3[at, :].astype(jnp.float32)
            there = jnp.where(core == 0, 2 * lax.div(i, 2) + lax.rem(unit, 2), lax.div(i, 2))
            k = lax.rem(there - other + 4, 4)
            to = pl.multiple_of((lax.rem(i, 2) * 8 + lax.div(unit, 2)) * UNIT, UNIT)
            blocks[k, pl.ds(to, UNIT), :] = total

        return filled + count

    lax.fori_loop(0, 8, one_sector, 0)
    keep_ref[...] = blocks[0]
    for k, dest in enumerate((send1, send2, send3)):
        dest[...] = blocks[k + 1].astype(jnp.bfloat16)


def regroup(rows, own, got):
    vmem = pl.BlockSpec(memory_space=pltpu.VMEM)
    send = jax.ShapeDtypeStruct((512, 256), jnp.bfloat16)
    return pl.pallas_call(
        regroup_kernel,
        out_shape=(jax.ShapeDtypeStruct((512, 256), jnp.float32), send, send, send),
        in_specs=[pl.BlockSpec(memory_space=pltpu.SMEM)] + [vmem] * 4,
        out_specs=(vmem,) * 4,
        scratch_shapes=[pltpu.VMEM((4, 512, 256), jnp.float32)],
        compiler_params=pltpu.CompilerParams(vmem_limit_bytes=32 * 1024 * 1024),
        name="regroup",
    )(rows, own, *got)


def spread_kernel(keep_ref, got1, got2, got3, out_ref):
    total = keep_ref[...] + got1[...].astype(jnp.float32)
    total = total + got2[...].astype(jnp.float32)
    total = (total + got3[...].astype(jnp.float32)).astype(jnp.bfloat16)
    for b in range(2):
        for z in range(8):
            for core in range(2):
                start = (b * 8 + z) * UNIT + core * 16
                out_ref[z * 2 + core, b] = total[start : start + 16]


def spread(keep, got):
    vmem = pl.BlockSpec(memory_space=pltpu.VMEM)
    return pl.pallas_call(
        spread_kernel,
        out_shape=jax.ShapeDtypeStruct((16, 2, 16, 256), jnp.bfloat16),
        in_specs=[vmem] * 4,
        out_specs=vmem,
        name="spread",
    )(keep, *got)


def finish_kernel(rows_ref, parts_ref, out_ref):
    term, sector = lax.axis_index("term"), lax.axis_index("sector")
    row = term * 16 + lax.broadcasted_iota(jnp.int32, (16, 1), 0)
    for b in range(2):
        used = row < rows_ref[2 * sector + b]
        for half in range(2):
            total = parts_ref[half, b].astype(jnp.float32)
            for z in range(1, 8):
                total = total + parts_ref[z * 2 + half, b].astype(jnp.float32)
            out_ref[b, :, half * 256 : half * 256 + 256] = jnp.where(used, total, jnp.zeros_like(total))


def finish(rows, parts):
    vmem = pl.BlockSpec(memory_space=pltpu.VMEM)
    return pl.pallas_call(
        finish_kernel,
        out_shape=jax.ShapeDtypeStruct((2, 16, 512), jnp.float32),
        in_specs=[pl.BlockSpec(memory_space=pltpu.SMEM), vmem],
        out_specs=vmem,
        name="finish",
    )(rows, parts)


def sized(sizes, wavefunction, left_operators, right_operators, small, sector_rows):
    wave_rows, group_rows = sizes[0] * UNIT, sizes[1] * UNIT
    send = functools.partial(lax.ppermute, axis_name=AXES)
    packed = pack_wave(sector_rows, wavefunction, wave_rows)
    got = [send(packed, perm=perm) for perm in GATHER_FIRST]
    far_small = send(jnp.concatenate(small), perm=OTHER_CORE)
    far_left = send(left_operators, perm=OTHER_CORE)
    far_right = send(right_operators, perm=OTHER_CORE)
    both, second, first = join(sector_rows, packed, got, group_rows)
    got = [send(block, perm=perm) for block, perm in zip((first, second, first), GATHER_SECOND)]
    near = [both, *got]
    far = [send(block, perm=OTHER_CORE) for block in near[:3]]
    far.append(send(near[3], perm=FROM_CORE_0))
    operators = (left_operators, right_operators, far_left, far_right)
    own, *sends = term_products(sector_rows, small, far_small, near, far, operators, group_rows)
    got = [send(s, perm=FIRST_AXIS[k + 1]) for k, s in enumerate(sends)]
    return regroup(sector_rows, own, got)


def local(
    wavefunction,
    left_operators,
    right_operators,
    source_sector,
    target_sector,
    live_terms,
    sector_rows,
):
    small = (source_sector, target_sector, live_terms)
    branches = [functools.partial(sized, sizes) for sizes in SIZES]
    operands = (wavefunction, left_operators, right_operators, small, sector_rows)
    keep, *sends = lax.switch(choose(sector_rows, SIZES), branches, *operands)
    got = [lax.ppermute(s, AXES, SECOND_AXIS[k + 1]) for k, s in enumerate(sends)]
    parts = spread(keep, got)
    groups = [[z * 4 + x_lo * 2 + core for z in range(8) for core in range(2)] for x_lo in range(2)]
    arrived = lax.all_to_all(
        parts, "term", split_axis=0, concat_axis=0, axis_index_groups=groups, tiled=True
    )
    return finish(sector_rows, arrived)


def solution(mesh):
    in_specs = (
        P("sector", None, None),
        P(("term", "sector"), None, None),
        P(("term", "sector"), None, None),
        P(("term", "sector")),
        P(("term", "sector")),
        P(("term", "sector")),
        P(),
    )
    out_specs = P("sector", "term", None)
    return jax.shard_map(local, mesh=mesh, in_specs=in_specs, out_specs=out_specs, check_vma=False)
```

```python
import functools

import jax
import jax.numpy as jnp
from jax import lax
from jax.experimental import pallas as pl
from jax.experimental.pallas import tpu as pltpu
from jax.sharding import PartitionSpec as P

UNIT = 32
AXES = ("term", "sector")
DEPTH = 3
SIZES = ((25, 38), (28, 44), (32, 64))


def device_index(x, y, z, core):
    x, y, z = x % 4, y % 4, z % 8
    return (z * 4 + (x % 2) * 2 + core) * 8 + y * 2 + x // 2


def pairs(move):
    every = [(x, y, z, c) for x in range(4) for y in range(4) for z in range(8) for c in range(2)]
    return [(device_index(*at), device_index(*move(*at))) for at in every if move(*at) is not None]


OTHER_CORE = pairs(lambda x, y, z, c: (x, y, z, 1 - c))
FIRST_AXIS = [pairs(lambda x, y, z, c: (x + k * c, y + k * (1 - c), z, c)) for k in range(4)]
ACROSS = (3, 2, 1, 0)
GATHER_FIRST = [
    pairs(lambda x, y, z, c: (x, y + 1, z, c) if c else (ACROSS[x], y, z, c)),
    pairs(lambda x, y, z, c: (x, y + 2, z, c) if c else None),
    pairs(lambda x, y, z, c: (x, y + 3, z, c) if c else None),
]
GATHER_SECOND = [
    pairs(lambda x, y, z, c: (ACROSS[x], y, z, c) if c else (x, y + 1, z, c)),
    pairs(lambda x, y, z, c: (ACROSS[x], y, z, c) if c else (x, y + 2, z, c)),
    pairs(lambda x, y, z, c: None if c else (x, y + 3, z, c)),
]
FROM_CORE_0 = pairs(lambda x, y, z, c: None if c else (x, y, z, 1))
SECOND_AXIS = [pairs(lambda x, y, z, c: (x + k * (1 - c), y + k * c, z, c)) for k in range(4)]


def coordinates():
    term, sector = lax.axis_index("term"), lax.axis_index("sector")
    x_lo, core = lax.rem(lax.div(term, 2), 2), lax.rem(term, 2)
    return 2 * lax.rem(sector, 2) + x_lo, lax.div(sector, 2), lax.div(term, 4), core


def units_of(rows):
    return lax.div(rows + (UNIT - 1), UNIT)


def group_entry(core, place, i):
    along_x = 4 * lax.div(i, 2) + 2 * lax.div(place, 2) + lax.rem(i, 2)
    sector = jnp.where(core == 0, 4 * place + lax.rem(i, 4), along_x)
    first = jnp.where(core == 0, 0, lax.rem(place, 2))
    return sector, first, 1 + core


def group_count(rows_ref, core, place, i):
    sector, first, step = group_entry(core, place, i)
    count = lax.div(units_of(rows_ref[sector]) - first + step - 1, step)
    return jnp.where((core == 0) & (i >= 4), 0, jnp.maximum(count, 0))


def unit_at(u):
    return pl.ds(pl.multiple_of(u * UNIT, UNIT), UNIT)


def choose_kernel(sizes, rows_ref, out_ref):
    units = [units_of(rows_ref[q]) for q in range(16)]
    pair = functools.reduce(jnp.maximum, [units[q] + units[q + 1] for q in range(0, 16, 2)])
    along_y = functools.reduce(jnp.maximum, [sum(units[q : q + 4]) for q in range(0, 16, 4)])
    along_x, across = jnp.int32(0), jnp.int32(0)
    for x_hi in range(2):
        mine = [units[q] for q in range(16) if (q // 2) % 2 == x_hi]
        across = jnp.maximum(across, sum(mine))
        along_x = jnp.maximum(along_x, sum(lax.div(n + 1, 2) for n in mine))
    group = jnp.maximum(jnp.maximum(along_y, along_x), lax.div(across + 1, 2))
    chosen = jnp.int32(len(sizes) - 1)
    for i in reversed(range(len(sizes) - 1)):
        chosen = jnp.where((pair <= sizes[i][0]) & (group <= sizes[i][1]), i, chosen)
    out_ref[0] = chosen


def choose(sector_rows, sizes):
    smem = pl.BlockSpec(memory_space=pltpu.SMEM)
    return pl.pallas_call(
        functools.partial(choose_kernel, sizes),
        out_shape=jax.ShapeDtypeStruct((1,), jnp.int32),
        in_specs=[smem],
        out_specs=smem,
        name="choose",
    )(sector_rows)[0]


def pack_kernel(rows_ref, wave_ref, out_ref):
    core = lax.rem(lax.axis_index("term"), 2)
    sector = lax.axis_index("sector")
    first_units = units_of(rows_ref[2 * sector])
    second_units = units_of(rows_ref[2 * sector + 1])

    def copy_half(half):
        lanes = pl.ds(half * 256, 256)
        for b, units, base in ((0, first_units, 0), (1, second_units, first_units)):

            @pl.loop(0, units)
            def _(u):
                out_ref[unit_at(base + u), :] = wave_ref[b, unit_at(u), lanes]

    for half in range(2):
        pl.when(core == half)(functools.partial(copy_half, half))


def pack_wave(sector_rows, wavefunction, rows):
    vmem = pl.BlockSpec(memory_space=pltpu.VMEM)
    return pl.pallas_call(
        pack_kernel,
        out_shape=jax.ShapeDtypeStruct((rows, 256), jnp.bfloat16),
        in_specs=[pl.BlockSpec(memory_space=pltpu.SMEM), vmem],
        out_specs=vmem,
        compiler_params=pltpu.CompilerParams(vmem_limit_bytes=16 * 1024 * 1024),
        name="pack_wave",
    )(sector_rows, wavefunction)


def join_kernel(rows_ref, own_ref, got1, got2, got3, both_ref, send2_ref, send1_ref):
    x, y, _, core = coordinates()
    x_hi = lax.div(x, 2)
    block_rows = send1_ref.shape[0]

    def one_pair(p, filled):
        pair = jnp.where(core == 0, 2 * y + p, 2 * p + x_hi)
        count = units_of(rows_ref[2 * pair]) + units_of(rows_ref[2 * pair + 1])
        count = jnp.where((core == 0) & (p >= 2), 0, count)
        from_x = jnp.where(p == x_hi, 0, 1)
        k = jnp.where(core == 0, from_x, lax.rem(y - p + 4, 4))
        for source, block in enumerate((own_ref, got1, got2, got3)):

            @pl.loop(0, jnp.where(k == source, count, 0))
            def _(u):
                both_ref[unit_at(filled + u), :] = block[unit_at(u), :]

        return filled + count

    lax.fori_loop(0, 4, one_pair, 0)
    send1_ref[...] = both_ref[:block_rows]

    @pl.when(core == 0)
    def _():
        send2_ref[...] = both_ref[:block_rows]

    @pl.when(core == 1)
    def _():
        send2_ref[...] = both_ref[block_rows:]


def join(sector_rows, own, got, rows):
    vmem = pl.BlockSpec(memory_space=pltpu.VMEM)
    block = jax.ShapeDtypeStruct((rows, 256), jnp.bfloat16)
    return pl.pallas_call(
        join_kernel,
        out_shape=(jax.ShapeDtypeStruct((2 * rows, 256), jnp.bfloat16), block, block),
        in_specs=[pl.BlockSpec(memory_space=pltpu.SMEM)] + [vmem] * 4,
        out_specs=(vmem,) * 3,
        compiler_params=pltpu.CompilerParams(vmem_limit_bytes=24 * 1024 * 1024),
        name="join",
    )(sector_rows, own, *got)


def terms_kernel(
    block_units,
    rows_ref,
    source_ref,
    target_ref,
    live_ref,
    far_source_ref,
    far_target_ref,
    far_live_ref,
    near0,
    near1,
    near2,
    near3,
    far0,
    far1,
    far2,
    far3,
    near_left,
    near_right,
    far_left,
    far_right,
    own_ref,
    send1,
    send2,
    send3,
    acc,
    left_buf,
    right_buf,
    wave_buf,
    half_buf,
    sems,
):
    x, y, _, core = coordinates()
    near_live = live_ref[0]
    total = near_live + far_live_ref[0]

    def facts(i):
        near = i < near_live
        slot = jnp.where(near, i, i - near_live)
        source = jnp.where(near, source_ref[slot], far_source_ref[slot])
        target = jnp.where(near, target_ref[slot], far_target_ref[slot])
        return near, slot, source, target

    def copies(near, slot, buf):
        left = near_left if near else far_left
        right = near_right if near else far_right
        lanes = pl.ds(pl.multiple_of(core * 256, 256), 256)
        return (
            pltpu.make_async_copy(left.at[slot], left_buf.at[buf], sems.at[buf, 0]),
            pltpu.make_async_copy(right.at[slot, lanes], right_buf.at[buf], sems.at[buf, 1]),
        )

    def begin(i):
        near, slot, _, _ = facts(i)
        buf = lax.rem(i, DEPTH)

        @pl.when(near)
        def _():
            for copy in copies(True, slot, buf):
                copy.start()

        @pl.when(jnp.logical_not(near))
        def _():
            for copy in copies(False, slot, buf):
                copy.start()

    for i in range(DEPTH - 1):
        pl.when(i < total)(functools.partial(begin, i))

    for q in range(16):

        @pl.loop(0, units_of(rows_ref[q]))
        def _(u):
            acc[unit_at(q * 16 + u), :] = jnp.zeros((UNIT, 256), jnp.float32)

    def fetch(source, units):
        source_y = lax.div(source, 4)
        pair = lax.div(source, 2)
        odd = lax.rem(source, 2)
        before_odd = jnp.where(odd == 1, units_of(rows_ref[2 * pair]), 0)
        k = lax.rem(y - source_y + 4, 4)
        before = jnp.where(
            lax.rem(pair, 2) == 1, units_of(rows_ref[4 * source_y]) + units_of(rows_ref[4 * source_y + 1]), 0
        )
        in_y = jnp.where(k == 0, 0, k + 1) * block_units + before + before_odd
        source_hi = lax.rem(pair, 2)
        before = before_odd
        for p in range(3):
            both = units_of(rows_ref[4 * p + 2 * source_hi]) + units_of(rows_ref[4 * p + 2 * source_hi + 1])
            before = before + jnp.where(p < source_y, both, 0)
        in_x = jnp.where(source_hi == lax.div(x, 2), 0, 2) * block_units + before
        for memory, layout, half in (
            ((near0, near1, near2, near3), core, core),
            ((far0, far1, far2, far3), 1 - core, 1 - core),
        ):
            first = jnp.where(layout == 0, in_y, in_x)
            low = 0
            for block in memory:
                high = low + block.shape[0] // UNIT
                begin_at, end_at = jnp.maximum(first, low), jnp.minimum(first + units, high)

                @pl.loop(begin_at, end_at)
                def _(u):
                    wave_buf[half, unit_at(u - first), :] = block[unit_at(u - low), :]

                low = high

    def clear_tail(source_rows, depth):
        last = units_of(source_rows) - 1
        keep = last * UNIT + lax.broadcasted_iota(jnp.int32, (UNIT, 256), 0) < source_rows
        for half in range(2):
            tile = wave_buf[half, unit_at(last), :]
            wave_buf[half, unit_at(last), :] = jnp.where(keep, tile, jnp.zeros_like(tile))

            @pl.loop(last + 1, depth // UNIT)
            def _(u):
                wave_buf[half, unit_at(u), :] = jnp.zeros((UNIT, 256), jnp.bfloat16)

    @pl.loop(0, total)
    def _(i):
        pl.when(i + DEPTH - 1 < total)(lambda: begin(i + DEPTH - 1))
        near, slot, source, target = facts(i)
        buf = lax.rem(i, DEPTH)
        source_rows = rows_ref[source]
        target_rows = rows_ref[target]
        fetch(source, units_of(source_rows))
        for copy in copies(True, slot, buf):
            copy.wait()

        def product(depth):
            clear_tail(source_rows, depth)

            @pl.loop(0, lax.div(target_rows + 255, 256))
            def _(part):
                rows = pl.ds(pl.multiple_of(part * 256, 256), 256)
                left = left_buf[buf, rows, pl.ds(0, depth)]
                for half in range(2):
                    wave = wave_buf[half, pl.ds(0, depth), :]
                    product = jnp.dot(left, wave, preferred_element_type=jnp.float32)
                    half_buf[:, half * 256 : half * 256 + 256] = product.astype(jnp.bfloat16)
                out = lax.dot_general(
                    half_buf[...], right_buf[buf], (((1,), (1,)), ((), ())), preferred_element_type=jnp.float32
                )
                acc[pl.ds(pl.multiple_of(target * 512 + part * 256, 256), 256), :] += out

        pl.when(source_rows <= 256)(functools.partial(product, 256))
        pl.when(source_rows > 256)(functools.partial(product, 512))

    place = jnp.where(core == 0, y, x)
    for k, dest in enumerate((own_ref, send1, send2, send3)):
        there = lax.rem(place + k, 4)

        def one_sector(i, filled):
            sector, first, step = group_entry(core, there, i)
            count = group_count(rows_ref, core, there, i)

            @pl.loop(0, count)
            def _(j):
                tile = acc[unit_at(sector * 16 + first + step * j), :]
                dest[unit_at(filled + j), :] = tile.astype(dest.dtype)

            return filled + count

        lax.fori_loop(0, 8, one_sector, 0)


def term_products(rows, small, far_small, near, far, operators, group_rows):
    smem = pl.BlockSpec(memory_space=pltpu.SMEM)
    hbm = pl.BlockSpec(memory_space=pltpu.HBM)
    vmem = pl.BlockSpec(memory_space=pltpu.VMEM)
    send = jax.ShapeDtypeStruct((group_rows, 256), jnp.bfloat16)
    return pl.pallas_call(
        functools.partial(terms_kernel, group_rows // UNIT),
        out_shape=(jax.ShapeDtypeStruct((group_rows, 256), jnp.float32), send, send, send),
        in_specs=[smem] * 7 + [vmem] * 8 + [hbm] * 4,
        out_specs=(vmem,) * 4,
        scratch_shapes=[
            pltpu.VMEM((16 * 512, 256), jnp.float32),
            pltpu.VMEM((DEPTH, 512, 512), jnp.bfloat16),
            pltpu.VMEM((DEPTH, 256, 512), jnp.bfloat16),
            pltpu.VMEM((2, 512, 256), jnp.bfloat16),
            pltpu.VMEM((256, 512), jnp.bfloat16),
            pltpu.SemaphoreType.DMA((DEPTH, 2)),
        ],
        compiler_params=pltpu.CompilerParams(vmem_limit_bytes=30 * 1024 * 1024),
        cost_estimate=pl.CostEstimate(flops=8 * 10**9, bytes_accessed=16 * 2**20, transcendentals=0),
        name="term_products",
    )(rows, *small, *far_small, *near, *far, *operators)


def regroup_kernel(rows_ref, own_ref, got1, got2, got3, keep_ref, send1, send2, send3, blocks):
    x, y, _, core = coordinates()
    place, other = jnp.where(core == 0, y, x), jnp.where(core == 0, x, y)
    blocks[...] = jnp.zeros_like(blocks)

    def one_sector(i, filled):
        _, first, step = group_entry(core, place, i)
        count = group_count(rows_ref, core, place, i)

        @pl.loop(0, count)
        def _(j):
            unit = first + step * j
            at = pl.ds(pl.multiple_of((filled + j) * UNIT, UNIT), UNIT)
            total = own_ref[at, :] + got1[at, :].astype(jnp.float32)
            total = total + got2[at, :].astype(jnp.float32)
            total = total + got3[at, :].astype(jnp.float32)
            there = jnp.where(core == 0, 2 * lax.div(i, 2) + lax.rem(unit, 2), lax.div(i, 2))
            k = lax.rem(there - other + 4, 4)
            to = pl.multiple_of((lax.rem(i, 2) * 8 + lax.div(unit, 2)) * UNIT, UNIT)
            blocks[k, pl.ds(to, UNIT), :] = total

        return filled + count

    lax.fori_loop(0, 8, one_sector, 0)
    keep_ref[...] = blocks[0]
    for k, dest in enumerate((send1, send2, send3)):
        dest[...] = blocks[k + 1].astype(jnp.bfloat16)


def regroup(rows, own, got):
    vmem = pl.BlockSpec(memory_space=pltpu.VMEM)
    send = jax.ShapeDtypeStruct((512, 256), jnp.bfloat16)
    return pl.pallas_call(
        regroup_kernel,
        out_shape=(jax.ShapeDtypeStruct((512, 256), jnp.float32), send, send, send),
        in_specs=[pl.BlockSpec(memory_space=pltpu.SMEM)] + [vmem] * 4,
        out_specs=(vmem,) * 4,
        scratch_shapes=[pltpu.VMEM((4, 512, 256), jnp.float32)],
        compiler_params=pltpu.CompilerParams(vmem_limit_bytes=32 * 1024 * 1024),
        name="regroup",
    )(rows, own, *got)


def spread_kernel(keep_ref, got1, got2, got3, out_ref):
    total = keep_ref[...] + got1[...].astype(jnp.float32)
    total = total + got2[...].astype(jnp.float32)
    total = (total + got3[...].astype(jnp.float32)).astype(jnp.bfloat16)
    for b in range(2):
        for z in range(8):
            start = (b * 8 + z) * UNIT
            out_ref[z, b] = total[start : start + UNIT]


def spread(keep, got):
    vmem = pl.BlockSpec(memory_space=pltpu.VMEM)
    return pl.pallas_call(
        spread_kernel,
        out_shape=jax.ShapeDtypeStruct((8, 2, UNIT, 256), jnp.bfloat16),
        in_specs=[vmem] * 4,
        out_specs=pl.BlockSpec(memory_space=pltpu.VMEM),
        name="spread",
    )(keep, *got)


def add_kernel(parts_ref, keep_ref, send_ref):
    core = lax.rem(lax.axis_index("term"), 2)
    for b in range(2):
        total = parts_ref[0, b].astype(jnp.float32)
        for z in range(1, 8):
            total = total + parts_ref[z, b].astype(jnp.float32)
        low, high = total[:16], total[16:]
        keep_ref[b] = jnp.where(core == 0, low, high)
        send_ref[b] = jnp.where(core == 0, high, low)


def add_parts(parts):
    vmem = pl.BlockSpec(memory_space=pltpu.VMEM)
    half = jax.ShapeDtypeStruct((2, 16, 256), jnp.float32)
    return pl.pallas_call(
        add_kernel, out_shape=(half, half), in_specs=[vmem], out_specs=(vmem, vmem), name="add_parts"
    )(parts)


def finish_kernel(rows_ref, keep_ref, got_ref, out_ref):
    term, sector = lax.axis_index("term"), lax.axis_index("sector")
    core = lax.rem(term, 2)
    row = term * 16 + lax.broadcasted_iota(jnp.int32, (16, 256), 0)
    for b in range(2):
        used = row < rows_ref[2 * sector + b]
        kept = jnp.where(used, keep_ref[b], 0.0)
        got = jnp.where(used, got_ref[b], 0.0)
        out_ref[b, :, :256] = jnp.where(core == 0, kept, got)
        out_ref[b, :, 256:] = jnp.where(core == 0, got, kept)


def finish(rows, keep, got):
    vmem = pl.BlockSpec(memory_space=pltpu.VMEM)
    return pl.pallas_call(
        finish_kernel,
        out_shape=jax.ShapeDtypeStruct((2, 16, 512), jnp.float32),
        in_specs=[pl.BlockSpec(memory_space=pltpu.SMEM), vmem, vmem],
        out_specs=vmem,
        name="finish",
    )(rows, keep, got)


def sized(sizes, wavefunction, left_operators, right_operators, small, sector_rows):
    wave_rows, group_rows = sizes[0] * UNIT, sizes[1] * UNIT
    send = functools.partial(lax.ppermute, axis_name=AXES)
    packed = pack_wave(sector_rows, wavefunction, wave_rows)
    got = [send(packed, perm=perm) for perm in GATHER_FIRST]
    far_small = [send(numbers, perm=OTHER_CORE) for numbers in small]
    far_left = send(left_operators, perm=OTHER_CORE)
    far_right = send(right_operators, perm=OTHER_CORE)
    both, second, first = join(sector_rows, packed, got, group_rows)
    got = [send(block, perm=perm) for block, perm in zip((first, second, first), GATHER_SECOND)]
    near = [both, *got]
    far = [send(block, perm=OTHER_CORE) for block in near[:3]]
    far.append(send(near[3], perm=FROM_CORE_0))
    operators = (left_operators, right_operators, far_left, far_right)
    own, *sends = term_products(sector_rows, small, far_small, near, far, operators, group_rows)
    got = [send(s, perm=FIRST_AXIS[k + 1]) for k, s in enumerate(sends)]
    return regroup(sector_rows, own, got)


def local(
    wavefunction,
    left_operators,
    right_operators,
    source_sector,
    target_sector,
    live_terms,
    sector_rows,
):
    small = (source_sector, target_sector, live_terms)
    branches = [functools.partial(sized, sizes) for sizes in SIZES]
    operands = (wavefunction, left_operators, right_operators, small, sector_rows)
    keep, *sends = lax.switch(choose(sector_rows, SIZES), branches, *operands)
    got = [lax.ppermute(s, AXES, SECOND_AXIS[k + 1]) for k, s in enumerate(sends)]
    parts = spread(keep, got)
    groups = [[z * 4 + place for z in range(8)] for place in range(4)]
    arrived = lax.all_to_all(
        parts, "term", split_axis=0, concat_axis=0, axis_index_groups=groups, tiled=True
    )
    keep, give = add_parts(arrived)
    return finish(sector_rows, keep, lax.ppermute(give, AXES, OTHER_CORE))


def solution(mesh):
    in_specs = (
        P("sector", None, None),
        P(("term", "sector"), None, None),
        P(("term", "sector"), None, None),
        P(("term", "sector")),
        P(("term", "sector")),
        P(("term", "sector")),
        P(),
    )
    out_specs = P("sector", "term", None)
    return jax.shard_map(local, mesh=mesh, in_specs=in_specs, out_specs=out_specs, check_vma=False)
```

```python
import functools

import jax
import jax.numpy as jnp
from jax import lax
from jax.experimental import pallas as pl
from jax.experimental.pallas import tpu as pltpu
from jax.sharding import PartitionSpec as P

UNIT = 32
TILE = 16
AXES = ("term", "sector")
DEPTH = 3
SIZES = ((25, 38), (28, 44), (32, 64))


def device_index(x, y, z, core):
    x, y, z = x % 4, y % 4, z % 8
    return (z * 4 + (x % 2) * 2 + core) * 8 + y * 2 + x // 2


def pairs(move):
    every = [(x, y, z, c) for x in range(4) for y in range(4) for z in range(8) for c in range(2)]
    return [(device_index(*at), device_index(*move(*at))) for at in every if move(*at) is not None]


OTHER_CORE = pairs(lambda x, y, z, c: (x, y, z, 1 - c))
FIRST_AXIS = [pairs(lambda x, y, z, c: (x + k * c, y + k * (1 - c), z, c)) for k in range(4)]
ACROSS = (3, 2, 1, 0)
GATHER_FIRST = [
    pairs(lambda x, y, z, c: (x, y + 1, z, c) if c else (ACROSS[x], y, z, c)),
    pairs(lambda x, y, z, c: (x, y + 2, z, c) if c else None),
    pairs(lambda x, y, z, c: (x, y + 3, z, c) if c else None),
]
GATHER_SECOND = [
    pairs(lambda x, y, z, c: (ACROSS[x], y, z, c) if c else (x, y + 1, z, c)),
    pairs(lambda x, y, z, c: (ACROSS[x], y, z, c) if c else (x, y + 2, z, c)),
    pairs(lambda x, y, z, c: None if c else (x, y + 3, z, c)),
]
FROM_CORE_0 = pairs(lambda x, y, z, c: None if c else (x, y, z, 1))
SECOND_AXIS = [pairs(lambda x, y, z, c: (x + k * (1 - c), y + k * c, z, c)) for k in range(4)]


def coordinates():
    term, sector = lax.axis_index("term"), lax.axis_index("sector")
    x_lo, core = lax.rem(lax.div(term, 2), 2), lax.rem(term, 2)
    return 2 * lax.rem(sector, 2) + x_lo, lax.div(sector, 2), lax.div(term, 4), core


def units_of(rows):
    return lax.div(rows + (UNIT - 1), UNIT)


def group_entry(core, place, i):
    along_x = 4 * lax.div(i, 2) + 2 * lax.div(place, 2) + lax.rem(i, 2)
    sector = jnp.where(core == 0, 4 * place + lax.rem(i, 4), along_x)
    first = jnp.where(core == 0, 0, lax.rem(place, 2))
    return sector, first, 1 + core


def group_count(rows_ref, core, place, i):
    sector, first, step = group_entry(core, place, i)
    count = lax.div(units_of(rows_ref[sector]) - first + step - 1, step)
    return jnp.where((core == 0) & (i >= 4), 0, jnp.maximum(count, 0))


def unit_at(u):
    return pl.ds(pl.multiple_of(u * UNIT, UNIT), UNIT)


def tile_at(u):
    return pl.ds(pl.multiple_of(u * TILE, TILE), TILE)


def choose_kernel(sizes, rows_ref, out_ref):
    units = [units_of(rows_ref[q]) for q in range(16)]
    pair = functools.reduce(jnp.maximum, [units[q] + units[q + 1] for q in range(0, 16, 2)])
    along_y = functools.reduce(jnp.maximum, [sum(units[q : q + 4]) for q in range(0, 16, 4)])
    along_x, across = jnp.int32(0), jnp.int32(0)
    for x_hi in range(2):
        mine = [units[q] for q in range(16) if (q // 2) % 2 == x_hi]
        across = jnp.maximum(across, sum(mine))
        along_x = jnp.maximum(along_x, sum(lax.div(n + 1, 2) for n in mine))
    group = jnp.maximum(jnp.maximum(along_y, along_x), lax.div(across + 1, 2))
    chosen = jnp.int32(len(sizes) - 1)
    for i in reversed(range(len(sizes) - 1)):
        chosen = jnp.where((pair <= sizes[i][0]) & (group <= sizes[i][1]), i, chosen)
    out_ref[0] = chosen


def choose(sector_rows, sizes):
    smem = pl.BlockSpec(memory_space=pltpu.SMEM)
    return pl.pallas_call(
        functools.partial(choose_kernel, sizes),
        out_shape=jax.ShapeDtypeStruct((1,), jnp.int32),
        in_specs=[smem],
        out_specs=smem,
        name="choose",
    )(sector_rows)[0]


def pack_kernel(rows_ref, wave_ref, out_ref):
    core = lax.rem(lax.axis_index("term"), 2)
    sector = lax.axis_index("sector")
    first_units = units_of(rows_ref[2 * sector])
    second_units = units_of(rows_ref[2 * sector + 1])

    def copy_half(half):
        lanes = pl.ds(half * 256, 256)
        for b, units, base in ((0, first_units, 0), (1, second_units, first_units)):

            @pl.loop(0, units)
            def _(u):
                out_ref[unit_at(base + u), :] = wave_ref[b, unit_at(u), lanes]

    for half in range(2):
        pl.when(core == half)(functools.partial(copy_half, half))


def pack_wave(sector_rows, wavefunction, rows):
    vmem = pl.BlockSpec(memory_space=pltpu.VMEM)
    return pl.pallas_call(
        pack_kernel,
        out_shape=jax.ShapeDtypeStruct((rows, 256), jnp.bfloat16),
        in_specs=[pl.BlockSpec(memory_space=pltpu.SMEM), vmem],
        out_specs=vmem,
        compiler_params=pltpu.CompilerParams(vmem_limit_bytes=16 * 1024 * 1024),
        name="pack_wave",
    )(sector_rows, wavefunction)


def join_kernel(rows_ref, own_ref, got1, got2, got3, both_ref, send2_ref, send1_ref):
    x, y, _, core = coordinates()
    x_hi = lax.div(x, 2)
    block_rows = send1_ref.shape[0]

    def one_pair(p, filled):
        pair = jnp.where(core == 0, 2 * y + p, 2 * p + x_hi)
        count = units_of(rows_ref[2 * pair]) + units_of(rows_ref[2 * pair + 1])
        count = jnp.where((core == 0) & (p >= 2), 0, count)
        from_x = jnp.where(p == x_hi, 0, 1)
        k = jnp.where(core == 0, from_x, lax.rem(y - p + 4, 4))
        for source, block in enumerate((own_ref, got1, got2, got3)):

            @pl.loop(0, jnp.where(k == source, count, 0))
            def _(u):
                both_ref[unit_at(filled + u), :] = block[unit_at(u), :]

        return filled + count

    lax.fori_loop(0, 4, one_pair, 0)
    send1_ref[...] = both_ref[:block_rows]

    @pl.when(core == 0)
    def _():
        send2_ref[...] = both_ref[:block_rows]

    @pl.when(core == 1)
    def _():
        send2_ref[...] = both_ref[block_rows:]


def join(sector_rows, own, got, rows):
    vmem = pl.BlockSpec(memory_space=pltpu.VMEM)
    block = jax.ShapeDtypeStruct((rows, 256), jnp.bfloat16)
    return pl.pallas_call(
        join_kernel,
        out_shape=(jax.ShapeDtypeStruct((2 * rows, 256), jnp.bfloat16), block, block),
        in_specs=[pl.BlockSpec(memory_space=pltpu.SMEM)] + [vmem] * 4,
        out_specs=(vmem,) * 3,
        compiler_params=pltpu.CompilerParams(vmem_limit_bytes=24 * 1024 * 1024),
        name="join",
    )(sector_rows, own, *got)


def terms_kernel(
    block_units,
    rows_ref,
    source_ref,
    target_ref,
    live_ref,
    far_source_ref,
    far_target_ref,
    far_live_ref,
    near0,
    near1,
    near2,
    near3,
    far0,
    far1,
    far2,
    far3,
    near_left,
    near_right,
    far_left,
    far_right,
    own_ref,
    send1,
    send2,
    send3,
    acc,
    left_buf,
    right_buf,
    wave_buf,
    sems,
):
    x, y, _, core = coordinates()
    near_live = live_ref[0]
    total = near_live + far_live_ref[0]

    def facts(i):
        near = i < near_live
        slot = jnp.where(near, i, i - near_live)
        source = jnp.where(near, source_ref[slot], far_source_ref[slot])
        target = jnp.where(near, target_ref[slot], far_target_ref[slot])
        return near, slot, source, target

    def copies(near, slot, buf):
        left = near_left if near else far_left
        right = near_right if near else far_right
        return (
            pltpu.make_async_copy(left.at[slot, :, core], left_buf.at[buf], sems.at[buf, 0]),
            pltpu.make_async_copy(right.at[slot], right_buf.at[buf], sems.at[buf, 1]),
        )

    def begin(i):
        near, slot, _, _ = facts(i)
        buf = lax.rem(i, DEPTH)

        @pl.when(near)
        def _():
            for copy in copies(True, slot, buf):
                copy.start()

        @pl.when(jnp.logical_not(near))
        def _():
            for copy in copies(False, slot, buf):
                copy.start()

    for i in range(DEPTH - 1):
        pl.when(i < total)(functools.partial(begin, i))

    for q in range(16):

        @pl.loop(0, units_of(rows_ref[q]))
        def _(u):
            acc[tile_at(q * 16 + u), :] = jnp.zeros((TILE, 512), jnp.float32)

    def fetch(source, units):
        source_y = lax.div(source, 4)
        pair = lax.div(source, 2)
        odd = lax.rem(source, 2)
        before_odd = jnp.where(odd == 1, units_of(rows_ref[2 * pair]), 0)
        k = lax.rem(y - source_y + 4, 4)
        before = jnp.where(
            lax.rem(pair, 2) == 1, units_of(rows_ref[4 * source_y]) + units_of(rows_ref[4 * source_y + 1]), 0
        )
        in_y = jnp.where(k == 0, 0, k + 1) * block_units + before + before_odd
        source_hi = lax.rem(pair, 2)
        before = before_odd
        for p in range(3):
            both = units_of(rows_ref[4 * p + 2 * source_hi]) + units_of(rows_ref[4 * p + 2 * source_hi + 1])
            before = before + jnp.where(p < source_y, both, 0)
        in_x = jnp.where(source_hi == lax.div(x, 2), 0, 2) * block_units + before
        for memory, layout, half in (
            ((near0, near1, near2, near3), core, core),
            ((far0, far1, far2, far3), 1 - core, 1 - core),
        ):
            first = jnp.where(layout == 0, in_y, in_x)
            low = 0
            for block in memory:
                high = low + block.shape[0] // UNIT
                begin_at, end_at = jnp.maximum(first, low), jnp.minimum(first + units, high)

                @pl.loop(begin_at, end_at)
                def _(u):
                    wave_buf[half, unit_at(u - first), :] = block[unit_at(u - low), :]

                low = high

    def clear_tail(source_rows, depth):
        last = units_of(source_rows) - 1
        keep = last * UNIT + lax.broadcasted_iota(jnp.int32, (UNIT, 256), 0) < source_rows
        for half in range(2):
            tile = wave_buf[half, unit_at(last), :]
            wave_buf[half, unit_at(last), :] = jnp.where(keep, tile, jnp.zeros_like(tile))

            @pl.loop(last + 1, depth // UNIT)
            def _(u):
                wave_buf[half, unit_at(u), :] = jnp.zeros((UNIT, 256), jnp.bfloat16)

    @pl.loop(0, total)
    def _(i):
        pl.when(i + DEPTH - 1 < total)(lambda: begin(i + DEPTH - 1))
        near, slot, source, target = facts(i)
        buf = lax.rem(i, DEPTH)
        source_rows = rows_ref[source]
        target_rows = rows_ref[target]
        fetch(source, units_of(source_rows))
        for copy in copies(True, slot, buf):
            copy.wait()

        def product(tiles, depth):
            left = left_buf[buf, pl.ds(0, tiles), :, pl.ds(0, depth)].reshape(tiles * TILE, depth)
            halves = []
            for half in range(2):
                part = jnp.dot(left, wave_buf[half, pl.ds(0, depth), :], preferred_element_type=jnp.float32)
                halves.append(part.astype(jnp.bfloat16))
            out = lax.dot_general(
                jnp.concatenate(halves, axis=1),
                right_buf[buf],
                (((1,), (1,)), ((), ())),
                preferred_element_type=jnp.float32,
            )
            acc[pl.ds(pl.multiple_of(target * 256, 256), tiles * TILE), :] += out

        for depth in (256, 512):

            @pl.when((source_rows <= 256) if depth == 256 else (source_rows > 256))
            def _():
                clear_tail(source_rows, depth)
                pl.when(target_rows <= 256)(functools.partial(product, 8, depth))
                pl.when(target_rows > 256)(functools.partial(product, 16, depth))

    place = jnp.where(core == 0, y, x)
    for k, dest in enumerate((own_ref, send1, send2, send3)):
        there = lax.rem(place + k, 4)

        def one_sector(i, filled):
            sector, first, step = group_entry(core, there, i)
            count = group_count(rows_ref, core, there, i)

            @pl.loop(0, count)
            def _(j):
                tile = acc[tile_at(sector * 16 + first + step * j), :]
                dest[tile_at(filled + j), :] = tile.astype(dest.dtype)

            return filled + count

        lax.fori_loop(0, 8, one_sector, 0)


def term_products(rows, small, far_small, near, far, operators, group_units):
    smem = pl.BlockSpec(memory_space=pltpu.SMEM)
    hbm = pl.BlockSpec(memory_space=pltpu.HBM)
    vmem = pl.BlockSpec(memory_space=pltpu.VMEM)
    send = jax.ShapeDtypeStruct((group_units * TILE, 512), jnp.bfloat16)
    return pl.pallas_call(
        functools.partial(terms_kernel, group_units),
        out_shape=(jax.ShapeDtypeStruct((group_units * TILE, 512), jnp.float32), send, send, send),
        in_specs=[smem] * 7 + [vmem] * 8 + [hbm] * 4,
        out_specs=(vmem,) * 4,
        scratch_shapes=[
            pltpu.VMEM((16 * 256, 512), jnp.float32),
            pltpu.VMEM((DEPTH, 16, TILE, 512), jnp.bfloat16),
            pltpu.VMEM((DEPTH, 512, 512), jnp.bfloat16),
            pltpu.VMEM((2, 512, 256), jnp.bfloat16),
            pltpu.SemaphoreType.DMA((DEPTH, 2)),
        ],
        compiler_params=pltpu.CompilerParams(vmem_limit_bytes=30 * 1024 * 1024),
        cost_estimate=pl.CostEstimate(flops=8 * 10**9, bytes_accessed=16 * 2**20, transcendentals=0),
        name="term_products",
    )(rows, *small, *far_small, *near, *far, *operators)


def regroup_kernel(rows_ref, own_ref, got1, got2, got3, keep_ref, send1, send2, send3, blocks):
    x, y, _, core = coordinates()
    place, other = jnp.where(core == 0, y, x), jnp.where(core == 0, x, y)
    blocks[...] = jnp.zeros_like(blocks)

    def one_sector(i, filled):
        _, first, step = group_entry(core, place, i)
        count = group_count(rows_ref, core, place, i)

        @pl.loop(0, count)
        def _(j):
            unit = first + step * j
            at = tile_at(filled + j)
            total = own_ref[at, :] + got1[at, :].astype(jnp.float32)
            total = total + got2[at, :].astype(jnp.float32)
            total = total + got3[at, :].astype(jnp.float32)
            there = jnp.where(core == 0, 2 * lax.div(i, 2) + lax.rem(unit, 2), lax.div(i, 2))
            k = lax.rem(there - other + 4, 4)
            blocks[k, tile_at(lax.rem(i, 2) * 8 + lax.div(unit, 2)), :] = total

        return filled + count

    lax.fori_loop(0, 8, one_sector, 0)
    keep_ref[...] = blocks[0]
    for k, dest in enumerate((send1, send2, send3)):
        dest[...] = blocks[k + 1].astype(jnp.bfloat16)


def regroup(rows, own, got):
    vmem = pl.BlockSpec(memory_space=pltpu.VMEM)
    send = jax.ShapeDtypeStruct((256, 512), jnp.bfloat16)
    return pl.pallas_call(
        regroup_kernel,
        out_shape=(jax.ShapeDtypeStruct((256, 512), jnp.float32), send, send, send),
        in_specs=[pl.BlockSpec(memory_space=pltpu.SMEM)] + [vmem] * 4,
        out_specs=(vmem,) * 4,
        scratch_shapes=[pltpu.VMEM((4, 256, 512), jnp.float32)],
        compiler_params=pltpu.CompilerParams(vmem_limit_bytes=24 * 1024 * 1024),
        name="regroup",
    )(rows, own, *got)


def spread_kernel(keep_ref, got1, got2, got3, out_ref):
    for b in range(2):
        for z in range(8):
            at = pl.ds((b * 8 + z) * TILE, TILE)
            total = keep_ref[at, :] + got1[at, :].astype(jnp.float32)
            total = total + got2[at, :].astype(jnp.float32)
            total = total + got3[at, :].astype(jnp.float32)
            out_ref[z, b] = total.astype(jnp.bfloat16)


def spread(keep, got):
    vmem = pl.BlockSpec(memory_space=pltpu.VMEM)
    return pl.pallas_call(
        spread_kernel,
        out_shape=jax.ShapeDtypeStruct((8, 2, TILE, 512), jnp.bfloat16),
        in_specs=[vmem] * 4,
        out_specs=vmem,
        name="spread",
    )(keep, *got)


def finish_kernel(rows_ref, parts_ref, out_ref):
    term, sector = lax.axis_index("term"), lax.axis_index("sector")
    row = term * TILE + lax.broadcasted_iota(jnp.int32, (TILE, 512), 0)
    for b in range(2):
        total = parts_ref[0, b].astype(jnp.float32)
        for z in range(1, 8):
            total = total + parts_ref[z, b].astype(jnp.float32)
        out_ref[b] = jnp.where(row < rows_ref[2 * sector + b], total, 0.0)


def finish(rows, parts):
    vmem = pl.BlockSpec(memory_space=pltpu.VMEM)
    return pl.pallas_call(
        finish_kernel,
        out_shape=jax.ShapeDtypeStruct((2, TILE, 512), jnp.float32),
        in_specs=[pl.BlockSpec(memory_space=pltpu.SMEM), vmem],
        out_specs=vmem,
        name="finish",
    )(rows, parts)


def sized(sizes, wavefunction, left_operators, right_operators, small, far_small, sector_rows):
    wave_rows, group_rows = sizes[0] * UNIT, sizes[1] * UNIT
    send = functools.partial(lax.ppermute, axis_name=AXES)
    packed = pack_wave(sector_rows, wavefunction, wave_rows)
    got = [send(packed, perm=perm) for perm in GATHER_FIRST]
    far_left = send(left_operators, perm=OTHER_CORE)
    far_right = send(right_operators, perm=OTHER_CORE)
    both, second, first = join(sector_rows, packed, got, group_rows)
    got = [send(block, perm=perm) for block, perm in zip((first, second, first), GATHER_SECOND)]
    near = [both, *got]
    far = [send(block, perm=OTHER_CORE) for block in near[:3]]
    far.append(send(near[3], perm=FROM_CORE_0))
    split = (8, 16, 2, TILE, 512)
    operators = (left_operators.reshape(split), right_operators, far_left.reshape(split), far_right)
    own, *sends = term_products(sector_rows, small, far_small, near, far, operators, sizes[1])
    got = [send(s, perm=FIRST_AXIS[k + 1]) for k, s in enumerate(sends)]
    return regroup(sector_rows, own, got)


def local(
    wavefunction,
    left_operators,
    right_operators,
    source_sector,
    target_sector,
    live_terms,
    sector_rows,
):
    small = (source_sector, target_sector, live_terms)
    branches = [functools.partial(sized, sizes) for sizes in SIZES]
    far_small = tuple(lax.ppermute(numbers, AXES, OTHER_CORE) for numbers in small)
    operands = (wavefunction, left_operators, right_operators, small, far_small, sector_rows)
    keep, *sends = lax.switch(choose(sector_rows, SIZES), branches, *operands)
    got = [lax.ppermute(s, AXES, SECOND_AXIS[k + 1]) for k, s in enumerate(sends)]
    parts = spread(keep, got)
    groups = [[z * 4 + place for z in range(8)] for place in range(4)]
    arrived = lax.all_to_all(
        parts, "term", split_axis=0, concat_axis=0, axis_index_groups=groups, tiled=True
    )
    return finish(sector_rows, arrived)


def solution(mesh):
    in_specs = (
        P("sector", None, None),
        P(("term", "sector"), None, None),
        P(("term", "sector"), None, None),
        P(("term", "sector")),
        P(("term", "sector")),
        P(("term", "sector")),
        P(),
    )
    out_specs = P("sector", "term", None)
    return jax.shard_map(local, mesh=mesh, in_specs=in_specs, out_specs=out_specs, check_vma=False)
```

```python
import functools

import jax
import jax.numpy as jnp
from jax import lax
from jax.experimental import pallas as pl
from jax.experimental.pallas import tpu as pltpu
from jax.sharding import PartitionSpec as P

UNIT = 32
TILE = 16
AXES = ("term", "sector")
DEPTH = 3
SIZES = ((21, 38), (25, 42), (29, 48), (32, 64))


def device_index(x, y, z, core):
    x, y, z = x % 4, y % 4, z % 8
    return (z * 4 + (x % 2) * 2 + core) * 8 + y * 2 + x // 2


def pairs(move):
    every = [(x, y, z, c) for x in range(4) for y in range(4) for z in range(8) for c in range(2)]
    return [(device_index(*at), device_index(*move(*at))) for at in every]


OTHER_CORE = pairs(lambda x, y, z, c: (x, y, z, 1 - c))
FIRST_AXIS = [
    pairs(lambda x, y, z, c: (x + 2, y, z, 1) if c else (x, y + 2, z, 0)),
    pairs(lambda x, y, z, c: (3 - x, y, z, 1) if c else (x, y + 1, z, 0)),
    pairs(lambda x, y, z, c: (x ^ 1, y, z, 1) if c else (x, y + 3, z, 0)),
]
SECOND_AXIS = [pairs(lambda x, y, z, c: (x + k * (1 - c), y + k * c, z, c)) for k in range(4)]


def coordinates():
    term, sector = lax.axis_index("term"), lax.axis_index("sector")
    x_lo, core = lax.rem(lax.div(term, 2), 2), lax.rem(term, 2)
    return 2 * lax.rem(sector, 2) + x_lo, lax.div(sector, 2), lax.div(term, 4), core


def units_of(rows):
    return lax.div(rows + (UNIT - 1), UNIT)


def group_entry(core, place, i):
    along_x = 4 * lax.div(i, 2) + 2 * lax.div(place, 2) + lax.rem(i, 2)
    sector = jnp.where(core == 0, 4 * place + lax.rem(i, 4), along_x)
    first = jnp.where(core == 0, 0, lax.rem(place, 2))
    return sector, first, 1 + core


def group_count(rows_ref, core, place, i):
    sector, first, step = group_entry(core, place, i)
    count = lax.div(units_of(rows_ref[sector]) - first + step - 1, step)
    return jnp.where((core == 0) & (i >= 4), 0, jnp.maximum(count, 0))


def unit_at(u):
    return pl.ds(pl.multiple_of(u * UNIT, UNIT), UNIT)


def tile_at(u):
    return pl.ds(pl.multiple_of(u * TILE, TILE), TILE)


def choose_kernel(sizes, rows_ref, out_ref):
    units = [units_of(rows_ref[q]) for q in range(16)]
    pair = functools.reduce(jnp.maximum, [units[q] + units[q + 1] for q in range(0, 16, 2)])
    along_y = functools.reduce(jnp.maximum, [sum(units[q : q + 4]) for q in range(0, 16, 4)])
    along_x = jnp.int32(0)
    for x_hi in range(2):
        mine = [units[q] for q in range(16) if (q // 2) % 2 == x_hi]
        along_x = jnp.maximum(along_x, sum(lax.div(n + 1, 2) for n in mine))
    group = jnp.maximum(along_y, along_x)
    chosen = jnp.int32(len(sizes) - 1)
    for i in reversed(range(len(sizes) - 1)):
        chosen = jnp.where((pair <= sizes[i][0]) & (group <= sizes[i][1]), i, chosen)
    out_ref[0] = chosen


def choose(sector_rows, sizes):
    smem = pl.BlockSpec(memory_space=pltpu.SMEM)
    return pl.pallas_call(
        functools.partial(choose_kernel, sizes),
        out_shape=jax.ShapeDtypeStruct((1,), jnp.int32),
        in_specs=[smem],
        out_specs=smem,
        name="choose",
    )(sector_rows)[0]


def pack_kernel(rows_ref, wave_ref, out_ref):
    core = lax.rem(lax.axis_index("term"), 2)
    sector = lax.axis_index("sector")
    first_units = units_of(rows_ref[2 * sector])
    second_units = units_of(rows_ref[2 * sector + 1])

    def copy_half(half):
        lanes = pl.ds(half * 256, 256)
        for b, units, base in ((0, first_units, 0), (1, second_units, first_units)):

            @pl.loop(0, units)
            def _(u):
                out_ref[unit_at(base + u), :] = wave_ref[b, unit_at(u), lanes]

    for half in range(2):
        pl.when(core == half)(functools.partial(copy_half, half))


def pack_wave(sector_rows, wavefunction, rows):
    vmem = pl.BlockSpec(memory_space=pltpu.VMEM)
    return pl.pallas_call(
        pack_kernel,
        out_shape=jax.ShapeDtypeStruct((rows, 256), jnp.bfloat16),
        in_specs=[pl.BlockSpec(memory_space=pltpu.SMEM), vmem],
        out_specs=vmem,
        compiler_params=pltpu.CompilerParams(vmem_limit_bytes=16 * 1024 * 1024),
        name="pack_wave",
    )(sector_rows, wavefunction)


def terms_kernel(
    ahead,
    rows_ref,
    near_wave,
    far_wave,
    near_left,
    near_right,
    far_left,
    far_right,
    first_dest,
    second_dest,
    acc,
    left_buf,
    right_buf,
    wave_buf,
    chosen,
    sems,
):
    x, y, _, core = coordinates()
    near_live = rows_ref[32]

    def is_mine(target):
        to_y = lax.rem(lax.div(target, 4) - y + 4, 4)
        far_y = (to_y == 1) | (to_y == 2)
        far_x = lax.rem(lax.div(target, 2), 2) != lax.div(x, 2)
        return jnp.where(core == 0, far_y, far_x) == ahead

    def note(i, found):
        near = i < near_live
        slot = jnp.where(near, i, i - near_live)
        mine = is_mine(rows_ref[jnp.where(near, 24, 41) + slot])

        @pl.when(mine)
        def _():
            chosen[found] = i

        return found + mine.astype(jnp.int32)

    total = lax.fori_loop(0, near_live + rows_ref[49], note, 0)

    def facts(i):
        i = chosen[i]
        near = i < near_live
        slot = jnp.where(near, i, i - near_live)
        source = rows_ref[jnp.where(near, 16, 33) + slot]
        target = rows_ref[jnp.where(near, 24, 41) + slot]
        return near, slot, source, target

    def copies(near, slot, buf):
        left = near_left if near else far_left
        right = near_right if near else far_right
        return (
            pltpu.make_async_copy(left.at[slot, :, core], left_buf.at[buf], sems.at[buf, 0]),
            pltpu.make_async_copy(right.at[slot], right_buf.at[buf], sems.at[buf, 1]),
        )

    def begin(i):
        near, slot, _, _ = facts(i)
        buf = lax.rem(i, DEPTH)

        @pl.when(near)
        def _():
            for copy in copies(True, slot, buf):
                copy.start()

        @pl.when(jnp.logical_not(near))
        def _():
            for copy in copies(False, slot, buf):
                copy.start()

    for i in range(DEPTH - 1):
        pl.when(i < total)(functools.partial(begin, i))

    for q in range(16):

        @pl.loop(0, jnp.where(is_mine(jnp.int32(q)), units_of(rows_ref[q]), 0))
        def _(u):
            acc[tile_at(q * 16 + u), :] = jnp.zeros((TILE, 512), jnp.float32)

    def fetch(source, units):
        pair = lax.div(source, 2)
        before = jnp.where(lax.rem(source, 2) == 1, units_of(rows_ref[2 * pair]), 0)
        first = pair * (near_wave.shape[0] // (8 * UNIT)) + before

        @pl.loop(0, units)
        def _(u):
            wave_buf[core, unit_at(u), :] = near_wave[unit_at(first + u), :]
            wave_buf[1 - core, unit_at(u), :] = far_wave[unit_at(first + u), :]

    def clear_tail(source_rows, depth):
        last = units_of(source_rows) - 1
        keep = last * UNIT + lax.broadcasted_iota(jnp.int32, (UNIT, 256), 0) < source_rows
        for half in range(2):
            tile = wave_buf[half, unit_at(last), :]
            wave_buf[half, unit_at(last), :] = jnp.where(keep, tile, jnp.zeros_like(tile))

            @pl.loop(last + 1, depth // UNIT)
            def _(u):
                wave_buf[half, unit_at(u), :] = jnp.zeros((UNIT, 256), jnp.bfloat16)

    @pl.loop(0, total)
    def _(i):
        pl.when(i + DEPTH - 1 < total)(lambda: begin(i + DEPTH - 1))
        near, slot, source, target = facts(i)
        buf = lax.rem(i, DEPTH)
        source_rows = rows_ref[source]
        target_rows = rows_ref[target]
        fetch(source, units_of(source_rows))
        for copy in copies(True, slot, buf):
            copy.wait()

        def product(tiles, depth):
            left = left_buf[buf, pl.ds(0, tiles), :, pl.ds(0, depth)].reshape(tiles * TILE, depth)
            halves = []
            for half in range(2):
                part = jnp.dot(left, wave_buf[half, pl.ds(0, depth), :], preferred_element_type=jnp.float32)
                halves.append(part.astype(jnp.bfloat16))
            out = lax.dot_general(
                jnp.concatenate(halves, axis=1),
                right_buf[buf],
                (((1,), (1,)), ((), ())),
                preferred_element_type=jnp.float32,
            )
            acc[pl.ds(pl.multiple_of(target * 256, 256), tiles * TILE), :] += out

        for depth in (256, 512):

            @pl.when((source_rows <= 256) if depth == 256 else (source_rows > 256))
            def _():
                clear_tail(source_rows, depth)
                pl.when(target_rows <= 256)(functools.partial(product, 8, depth))
                pl.when(target_rows > 256)(functools.partial(product, 16, depth))

    if ahead:
        places = (lax.rem(jnp.where(core == 0, y, x) + 2, 4), jnp.where(core == 0, lax.rem(y + 1, 4), 3 - x))
    else:
        places = (jnp.where(core == 0, lax.rem(y + 3, 4), x + 1 - 2 * lax.rem(x, 2)), jnp.where(core == 0, y, x))
    for there, dest in zip(places, (first_dest, second_dest)):

        def one_sector(i, filled):
            sector, first, step = group_entry(core, there, i)
            count = group_count(rows_ref, core, there, i)

            @pl.loop(0, count)
            def _(j):
                tile = acc[tile_at(sector * 16 + first + step * j), :]
                dest[tile_at(filled + j), :] = tile.astype(dest.dtype)

            return filled + count

        lax.fori_loop(0, 8, one_sector, 0)


def term_products(numbers, near, far, operators, group_units, ahead):
    smem = pl.BlockSpec(memory_space=pltpu.SMEM)
    hbm = pl.BlockSpec(memory_space=pltpu.HBM)
    vmem = pl.BlockSpec(memory_space=pltpu.VMEM)
    send = jax.ShapeDtypeStruct((group_units * TILE, 512), jnp.bfloat16)
    last = send if ahead else jax.ShapeDtypeStruct((group_units * TILE, 512), jnp.float32)
    return pl.pallas_call(
        functools.partial(terms_kernel, ahead),
        out_shape=(send, last),
        in_specs=[smem] + [vmem] * 2 + [hbm] * 4,
        out_specs=(vmem,) * 2,
        scratch_shapes=[
            pltpu.VMEM((16 * 256, 512), jnp.float32),
            pltpu.VMEM((DEPTH, 16, TILE, 512), jnp.bfloat16),
            pltpu.VMEM((DEPTH, 512, 512), jnp.bfloat16),
            pltpu.VMEM((2, 512, 256), jnp.bfloat16),
            pltpu.SMEM((16,), jnp.int32),
            pltpu.SemaphoreType.DMA((DEPTH, 2)),
        ],
        compiler_params=pltpu.CompilerParams(vmem_limit_bytes=46 * 1024 * 1024),
        cost_estimate=pl.CostEstimate(flops=4 * 10**9, bytes_accessed=8 * 2**20, transcendentals=0),
        name="terms_ahead" if ahead else "terms_here",
    )(numbers, near, far, *operators)


def regroup_kernel(rows_ref, own_ref, got1, got2, got3, keep_ref, send1, send2, send3, blocks):
    x, y, _, core = coordinates()
    place, other = jnp.where(core == 0, y, x), jnp.where(core == 0, x, y)
    blocks[...] = jnp.zeros_like(blocks)

    def one_sector(i, filled):
        _, first, step = group_entry(core, place, i)
        count = group_count(rows_ref, core, place, i)

        @pl.loop(0, count)
        def _(j):
            unit = first + step * j
            at = tile_at(filled + j)
            total = own_ref[at, :] + got1[at, :].astype(jnp.float32)
            total = total + got2[at, :].astype(jnp.float32)
            total = total + got3[at, :].astype(jnp.float32)
            there = jnp.where(core == 0, 2 * lax.div(i, 2) + lax.rem(unit, 2), lax.div(i, 2))
            k = lax.rem(there - other + 4, 4)
            blocks[k, tile_at(lax.rem(i, 2) * 8 + lax.div(unit, 2)), :] = total

        return filled + count

    lax.fori_loop(0, 8, one_sector, 0)
    keep_ref[...] = blocks[0]
    for k, dest in enumerate((send1, send2, send3)):
        dest[...] = blocks[k + 1].astype(jnp.bfloat16)


def regroup(rows, own, got):
    vmem = pl.BlockSpec(memory_space=pltpu.VMEM)
    send = jax.ShapeDtypeStruct((256, 512), jnp.bfloat16)
    return pl.pallas_call(
        regroup_kernel,
        out_shape=(jax.ShapeDtypeStruct((256, 512), jnp.float32), send, send, send),
        in_specs=[pl.BlockSpec(memory_space=pltpu.SMEM)] + [vmem] * 4,
        out_specs=(vmem,) * 4,
        scratch_shapes=[pltpu.VMEM((4, 256, 512), jnp.float32)],
        compiler_params=pltpu.CompilerParams(vmem_limit_bytes=24 * 1024 * 1024),
        name="regroup",
    )(rows, own, *got)


def spread_kernel(keep_ref, got1, got2, got3, out_ref):
    for b in range(2):
        for z in range(8):
            at = pl.ds((b * 8 + z) * TILE, TILE)
            total = keep_ref[at, :] + got1[at, :].astype(jnp.float32)
            total = total + got2[at, :].astype(jnp.float32)
            total = total + got3[at, :].astype(jnp.float32)
            out_ref[z, b] = total.astype(jnp.bfloat16)


def spread(keep, got):
    vmem = pl.BlockSpec(memory_space=pltpu.VMEM)
    return pl.pallas_call(
        spread_kernel,
        out_shape=jax.ShapeDtypeStruct((8, 2, TILE, 512), jnp.bfloat16),
        in_specs=[vmem] * 4,
        out_specs=vmem,
        name="spread",
    )(keep, *got)


def finish_kernel(rows_ref, parts_ref, out_ref):
    term, sector = lax.axis_index("term"), lax.axis_index("sector")
    row = term * TILE + lax.broadcasted_iota(jnp.int32, (TILE, 512), 0)
    for b in range(2):
        total = parts_ref[0, b].astype(jnp.float32)
        for z in range(1, 8):
            total = total + parts_ref[z, b].astype(jnp.float32)
        out_ref[b] = jnp.where(row < rows_ref[2 * sector + b], total, 0.0)


def finish(rows, parts):
    vmem = pl.BlockSpec(memory_space=pltpu.VMEM)
    return pl.pallas_call(
        finish_kernel,
        out_shape=jax.ShapeDtypeStruct((2, TILE, 512), jnp.float32),
        in_specs=[pl.BlockSpec(memory_space=pltpu.SMEM), vmem],
        out_specs=vmem,
        name="finish",
    )(rows, parts)


def sized(sizes, wavefunction, left_operators, right_operators, small, far_small, sector_rows):
    send = functools.partial(lax.ppermute, axis_name=AXES)
    packed = pack_wave(sector_rows, wavefunction, sizes[0] * UNIT)
    packed = jnp.broadcast_to(packed, (8, *packed.shape))
    far_left = send(left_operators, perm=OTHER_CORE)
    far_right = send(right_operators, perm=OTHER_CORE)
    near = lax.all_to_all(packed, "sector", split_axis=0, concat_axis=0, tiled=True).reshape(-1, 256)
    far = send(near, perm=OTHER_CORE)
    split = (8, 16, 2, TILE, 512)
    operators = (left_operators.reshape(split), right_operators, far_left.reshape(split), far_right)
    numbers = jnp.concatenate([sector_rows, *small, *far_small])
    terms = functools.partial(term_products, numbers, near, far, operators, sizes[1])
    got = [send(block, perm=perm) for block, perm in zip(terms(True), FIRST_AXIS)]
    last, own = terms(False)
    got.append(send(last, perm=FIRST_AXIS[2]))
    return regroup(sector_rows, own, got)


def local(
    wavefunction,
    left_operators,
    right_operators,
    source_sector,
    target_sector,
    live_terms,
    sector_rows,
):
    small = (source_sector, target_sector, live_terms)
    branches = [functools.partial(sized, sizes) for sizes in SIZES]
    far_small = tuple(lax.ppermute(numbers, AXES, OTHER_CORE) for numbers in small)
    operands = (wavefunction, left_operators, right_operators, small, far_small, sector_rows)
    keep, *sends = lax.switch(choose(sector_rows, SIZES), branches, *operands)
    got = [lax.ppermute(s, AXES, SECOND_AXIS[k + 1]) for k, s in enumerate(sends)]
    parts = spread(keep, got)
    groups = [[z * 4 + place for z in range(8)] for place in range(4)]
    arrived = lax.all_to_all(
        parts, "term", split_axis=0, concat_axis=0, axis_index_groups=groups, tiled=True
    )
    return finish(sector_rows, arrived)


def solution(mesh):
    in_specs = (
        P("sector", None, None),
        P(("term", "sector"), None, None),
        P(("term", "sector"), None, None),
        P(("term", "sector")),
        P(("term", "sector")),
        P(("term", "sector")),
        P(),
    )
    out_specs = P("sector", "term", None)
    return jax.shard_map(local, mesh=mesh, in_specs=in_specs, out_specs=out_specs, check_vma=False)
```

```python
import functools

import jax
import jax.numpy as jnp
from jax import lax
from jax.experimental import pallas as pl
from jax.experimental.pallas import tpu as pltpu
from jax.sharding import PartitionSpec as P

UNIT = 32
TILE = 16
AXES = ("term", "sector")
DEPTH = 3
SIZES = ((21, 38), (25, 42), (29, 48), (32, 64))


def device_index(x, y, z, core):
    x, y, z = x % 4, y % 4, z % 8
    return (z * 4 + (x % 2) * 2 + core) * 8 + y * 2 + x // 2


def pairs(move):
    every = [(x, y, z, c) for x in range(4) for y in range(4) for z in range(8) for c in range(2)]
    return [(device_index(*at), device_index(*move(*at))) for at in every]


OTHER_CORE = pairs(lambda x, y, z, c: (x, y, z, 1 - c))
GATHER_GROUPS = [
    [device_index(x if x_hi == x // 2 else 3 - x, y, z, core) for y in range(4) for x_hi in range(2)]
    for x in range(2)
    for z in range(8)
    for core in range(2)
]
FIRST_AXIS = [
    pairs(lambda x, y, z, c: (x + 2, y, z, 1) if c else (x, y + 2, z, 0)),
    pairs(lambda x, y, z, c: (3 - x, y, z, 1) if c else (x, y + 1, z, 0)),
    pairs(lambda x, y, z, c: (x ^ 1, y, z, 1) if c else (x, y + 3, z, 0)),
]
SECOND_AXIS = [pairs(lambda x, y, z, c: (x + k * (1 - c), y + k * c, z, c)) for k in range(4)]


def coordinates():
    term, sector = lax.axis_index("term"), lax.axis_index("sector")
    x_lo, core = lax.rem(lax.div(term, 2), 2), lax.rem(term, 2)
    return 2 * lax.rem(sector, 2) + x_lo, lax.div(sector, 2), lax.div(term, 4), core


def units_of(rows):
    return lax.div(rows + (UNIT - 1), UNIT)


def group_entry(core, place, i):
    along_x = 4 * lax.div(i, 2) + 2 * lax.div(place, 2) + lax.rem(i, 2)
    sector = jnp.where(core == 0, 4 * place + lax.rem(i, 4), along_x)
    first = jnp.where(core == 0, 0, lax.rem(place, 2))
    return sector, first, 1 + core


def group_count(rows_ref, core, place, i):
    sector, first, step = group_entry(core, place, i)
    count = lax.div(units_of(rows_ref[sector]) - first + step - 1, step)
    return jnp.where((core == 0) & (i >= 4), 0, jnp.maximum(count, 0))


def unit_at(u):
    return pl.ds(pl.multiple_of(u * UNIT, UNIT), UNIT)


def tile_at(u):
    return pl.ds(pl.multiple_of(u * TILE, TILE), TILE)


def choose_kernel(sizes, rows_ref, out_ref):
    units = [units_of(rows_ref[q]) for q in range(16)]
    pair = functools.reduce(jnp.maximum, [units[q] + units[q + 1] for q in range(0, 16, 2)])
    along_y = functools.reduce(jnp.maximum, [sum(units[q : q + 4]) for q in range(0, 16, 4)])
    along_x = jnp.int32(0)
    for x_hi in range(2):
        mine = [units[q] for q in range(16) if (q // 2) % 2 == x_hi]
        along_x = jnp.maximum(along_x, sum(lax.div(n + 1, 2) for n in mine))
    group = jnp.maximum(along_y, along_x)
    chosen = jnp.int32(len(sizes) - 1)
    for i in reversed(range(len(sizes) - 1)):
        chosen = jnp.where((pair <= sizes[i][0]) & (group <= sizes[i][1]), i, chosen)
    out_ref[0] = chosen


def choose(sector_rows, sizes):
    smem = pl.BlockSpec(memory_space=pltpu.SMEM)
    return pl.pallas_call(
        functools.partial(choose_kernel, sizes),
        out_shape=jax.ShapeDtypeStruct((1,), jnp.int32),
        in_specs=[smem],
        out_specs=smem,
        name="choose",
    )(sector_rows)[0]


def pack_kernel(rows_ref, wave_ref, out_ref):
    core = lax.rem(lax.axis_index("term"), 2)
    sector = lax.axis_index("sector")
    first_units = units_of(rows_ref[2 * sector])
    second_units = units_of(rows_ref[2 * sector + 1])

    def copy_half(half):
        lanes = pl.ds(half * 256, 256)
        for b, units, base in ((0, first_units, 0), (1, second_units, first_units)):

            @pl.loop(0, units)
            def _(u):
                out_ref[unit_at(base + u), :] = wave_ref[b, unit_at(u), lanes]

    for half in range(2):
        pl.when(core == half)(functools.partial(copy_half, half))


def pack_wave(sector_rows, wavefunction, rows):
    vmem = pl.BlockSpec(memory_space=pltpu.VMEM)
    return pl.pallas_call(
        pack_kernel,
        out_shape=jax.ShapeDtypeStruct((rows, 256), jnp.bfloat16),
        in_specs=[pl.BlockSpec(memory_space=pltpu.SMEM), vmem],
        out_specs=vmem,
        compiler_params=pltpu.CompilerParams(vmem_limit_bytes=16 * 1024 * 1024),
        name="pack_wave",
    )(sector_rows, wavefunction)


def terms_kernel(
    ahead,
    rows_ref,
    near_wave,
    far_wave,
    near_left,
    near_right,
    far_left,
    far_right,
    first_dest,
    second_dest,
    acc,
    left_buf,
    right_buf,
    wave_buf,
    chosen,
    sems,
):
    x, y, _, core = coordinates()
    near_live = rows_ref[32]

    def is_mine(target):
        to_y = lax.rem(lax.div(target, 4) - y + 4, 4)
        far_y = (to_y == 1) | (to_y == 2)
        far_x = lax.rem(lax.div(target, 2), 2) != lax.div(x, 2)
        return jnp.where(core == 0, far_y, far_x) == ahead

    def note(i, found):
        near = i < near_live
        slot = jnp.where(near, i, i - near_live)
        mine = is_mine(rows_ref[jnp.where(near, 24, 41) + slot])

        @pl.when(mine)
        def _():
            chosen[found] = i

        return found + mine.astype(jnp.int32)

    total = lax.fori_loop(0, near_live + rows_ref[49], note, 0)

    def facts(i):
        i = chosen[i]
        near = i < near_live
        slot = jnp.where(near, i, i - near_live)
        source = rows_ref[jnp.where(near, 16, 33) + slot]
        target = rows_ref[jnp.where(near, 24, 41) + slot]
        return near, slot, source, target

    def copies(near, slot, buf):
        left = near_left if near else far_left
        right = near_right if near else far_right
        return (
            pltpu.make_async_copy(left.at[slot, :, core], left_buf.at[buf], sems.at[buf, 0]),
            pltpu.make_async_copy(right.at[slot], right_buf.at[buf], sems.at[buf, 1]),
        )

    def begin(i):
        near, slot, _, _ = facts(i)
        buf = lax.rem(i, DEPTH)

        @pl.when(near)
        def _():
            for copy in copies(True, slot, buf):
                copy.start()

        @pl.when(jnp.logical_not(near))
        def _():
            for copy in copies(False, slot, buf):
                copy.start()

    for i in range(DEPTH - 1):
        pl.when(i < total)(functools.partial(begin, i))

    for q in range(16):

        @pl.loop(0, jnp.where(is_mine(jnp.int32(q)), units_of(rows_ref[q]), 0))
        def _(u):
            acc[tile_at(q * 16 + u), :] = jnp.zeros((TILE, 512), jnp.float32)

    def fetch(source, units):
        pair = lax.div(source, 2)
        before = jnp.where(lax.rem(source, 2) == 1, units_of(rows_ref[2 * pair]), 0)
        first = pair * (near_wave.shape[0] // (8 * UNIT)) + before

        @pl.loop(0, units)
        def _(u):
            wave_buf[core, unit_at(u), :] = near_wave[unit_at(first + u), :]
            wave_buf[1 - core, unit_at(u), :] = far_wave[unit_at(first + u), :]

    def clear_tail(source_rows, depth):
        last = units_of(source_rows) - 1
        keep = last * UNIT + lax.broadcasted_iota(jnp.int32, (UNIT, 256), 0) < source_rows
        for half in range(2):
            tile = wave_buf[half, unit_at(last), :]
            wave_buf[half, unit_at(last), :] = jnp.where(keep, tile, jnp.zeros_like(tile))

            @pl.loop(last + 1, depth // UNIT)
            def _(u):
                wave_buf[half, unit_at(u), :] = jnp.zeros((UNIT, 256), jnp.bfloat16)

    @pl.loop(0, total)
    def _(i):
        pl.when(i + DEPTH - 1 < total)(lambda: begin(i + DEPTH - 1))
        near, slot, source, target = facts(i)
        buf = lax.rem(i, DEPTH)
        source_rows = rows_ref[source]
        target_rows = rows_ref[target]
        fetch(source, units_of(source_rows))
        for copy in copies(True, slot, buf):
            copy.wait()

        def product(tiles, depth):
            left = left_buf[buf, pl.ds(0, tiles), :, pl.ds(0, depth)].reshape(tiles * TILE, depth)
            halves = []
            for half in range(2):
                part = jnp.dot(left, wave_buf[half, pl.ds(0, depth), :], preferred_element_type=jnp.float32)
                halves.append(part.astype(jnp.bfloat16))
            out = lax.dot_general(
                jnp.concatenate(halves, axis=1),
                right_buf[buf],
                (((1,), (1,)), ((), ())),
                preferred_element_type=jnp.float32,
            )
            acc[pl.ds(pl.multiple_of(target * 256, 256), tiles * TILE), :] += out

        for depth in (256, 512):

            @pl.when((source_rows <= 256) if depth == 256 else (source_rows > 256))
            def _():
                clear_tail(source_rows, depth)
                pl.when(target_rows <= 256)(functools.partial(product, 8, depth))
                pl.when(target_rows > 256)(functools.partial(product, 16, depth))

    if ahead:
        places = (lax.rem(jnp.where(core == 0, y, x) + 2, 4), jnp.where(core == 0, lax.rem(y + 1, 4), 3 - x))
    else:
        places = (jnp.where(core == 0, lax.rem(y + 3, 4), x + 1 - 2 * lax.rem(x, 2)), jnp.where(core == 0, y, x))
    for there, dest in zip(places, (first_dest, second_dest)):

        def one_sector(i, filled):
            sector, first, step = group_entry(core, there, i)
            count = group_count(rows_ref, core, there, i)

            @pl.loop(0, count)
            def _(j):
                tile = acc[tile_at(sector * 16 + first + step * j), :]
                dest[tile_at(filled + j), :] = tile.astype(dest.dtype)

            return filled + count

        lax.fori_loop(0, 8, one_sector, 0)


def term_products(numbers, near, far, operators, group_units, ahead):
    smem = pl.BlockSpec(memory_space=pltpu.SMEM)
    hbm = pl.BlockSpec(memory_space=pltpu.HBM)
    vmem = pl.BlockSpec(memory_space=pltpu.VMEM)
    send = jax.ShapeDtypeStruct((group_units * TILE, 512), jnp.bfloat16)
    last = send if ahead else jax.ShapeDtypeStruct((group_units * TILE, 512), jnp.float32)
    return pl.pallas_call(
        functools.partial(terms_kernel, ahead),
        out_shape=(send, last),
        in_specs=[smem] + [vmem] * 2 + [hbm] * 4,
        out_specs=(vmem,) * 2,
        scratch_shapes=[
            pltpu.VMEM((16 * 256, 512), jnp.float32),
            pltpu.VMEM((DEPTH, 16, TILE, 512), jnp.bfloat16),
            pltpu.VMEM((DEPTH, 512, 512), jnp.bfloat16),
            pltpu.VMEM((2, 512, 256), jnp.bfloat16),
            pltpu.SMEM((16,), jnp.int32),
            pltpu.SemaphoreType.DMA((DEPTH, 2)),
        ],
        compiler_params=pltpu.CompilerParams(vmem_limit_bytes=46 * 1024 * 1024),
        cost_estimate=pl.CostEstimate(flops=4 * 10**9, bytes_accessed=8 * 2**20, transcendentals=0),
        name="terms_ahead" if ahead else "terms_here",
    )(numbers, near, far, *operators)


def regroup_kernel(rows_ref, own_ref, got1, got2, got3, keep_ref, send1, send2, send3, blocks):
    x, y, _, core = coordinates()
    place, other = jnp.where(core == 0, y, x), jnp.where(core == 0, x, y)
    blocks[...] = jnp.zeros_like(blocks)

    def one_sector(i, filled):
        _, first, step = group_entry(core, place, i)
        count = group_count(rows_ref, core, place, i)

        @pl.loop(0, count)
        def _(j):
            unit = first + step * j
            at = tile_at(filled + j)
            total = own_ref[at, :] + got1[at, :].astype(jnp.float32)
            total = total + got2[at, :].astype(jnp.float32)
            total = total + got3[at, :].astype(jnp.float32)
            there = jnp.where(core == 0, 2 * lax.div(i, 2) + lax.rem(unit, 2), lax.div(i, 2))
            k = lax.rem(there - other + 4, 4)
            blocks[k, tile_at(lax.rem(i, 2) * 8 + lax.div(unit, 2)), :] = total

        return filled + count

    lax.fori_loop(0, 8, one_sector, 0)
    keep_ref[...] = blocks[0]
    for k, dest in enumerate((send1, send2, send3)):
        dest[...] = blocks[k + 1].astype(jnp.bfloat16)


def regroup(rows, own, got):
    vmem = pl.BlockSpec(memory_space=pltpu.VMEM)
    send = jax.ShapeDtypeStruct((256, 512), jnp.bfloat16)
    return pl.pallas_call(
        regroup_kernel,
        out_shape=(jax.ShapeDtypeStruct((256, 512), jnp.float32), send, send, send),
        in_specs=[pl.BlockSpec(memory_space=pltpu.SMEM)] + [vmem] * 4,
        out_specs=(vmem,) * 4,
        scratch_shapes=[pltpu.VMEM((4, 256, 512), jnp.float32)],
        compiler_params=pltpu.CompilerParams(vmem_limit_bytes=24 * 1024 * 1024),
        name="regroup",
    )(rows, own, *got)


def spread_kernel(keep_ref, got1, got2, got3, out_ref):
    for b in range(2):
        for z in range(8):
            at = pl.ds((b * 8 + z) * TILE, TILE)
            total = keep_ref[at, :] + got1[at, :].astype(jnp.float32)
            total = total + got2[at, :].astype(jnp.float32)
            total = total + got3[at, :].astype(jnp.float32)
            out_ref[z, b] = total.astype(jnp.bfloat16)


def spread(keep, got):
    vmem = pl.BlockSpec(memory_space=pltpu.VMEM)
    return pl.pallas_call(
        spread_kernel,
        out_shape=jax.ShapeDtypeStruct((8, 2, TILE, 512), jnp.bfloat16),
        in_specs=[vmem] * 4,
        out_specs=vmem,
        name="spread",
    )(keep, *got)


def finish_kernel(rows_ref, parts_ref, out_ref):
    term, sector = lax.axis_index("term"), lax.axis_index("sector")
    row = term * TILE + lax.broadcasted_iota(jnp.int32, (TILE, 512), 0)
    for b in range(2):
        total = parts_ref[0, b].astype(jnp.float32)
        for z in range(1, 8):
            total = total + parts_ref[z, b].astype(jnp.float32)
        out_ref[b] = jnp.where(row < rows_ref[2 * sector + b], total, 0.0)


def finish(rows, parts):
    vmem = pl.BlockSpec(memory_space=pltpu.VMEM)
    return pl.pallas_call(
        finish_kernel,
        out_shape=jax.ShapeDtypeStruct((2, TILE, 512), jnp.float32),
        in_specs=[pl.BlockSpec(memory_space=pltpu.SMEM), vmem],
        out_specs=vmem,
        name="finish",
    )(rows, parts)


def sized(sizes, wavefunction, left_operators, right_operators, small, far_small, sector_rows):
    send = functools.partial(lax.ppermute, axis_name=AXES)
    packed = pack_wave(sector_rows, wavefunction, sizes[0] * UNIT)
    packed = jnp.broadcast_to(packed, (8, *packed.shape))
    far_left = send(left_operators, perm=OTHER_CORE)
    far_right = send(right_operators, perm=OTHER_CORE)
    near = lax.all_to_all(
        packed, AXES, split_axis=0, concat_axis=0, axis_index_groups=GATHER_GROUPS, tiled=True
    ).reshape(-1, 256)
    far = send(near, perm=OTHER_CORE)
    split = (8, 16, 2, TILE, 512)
    operators = (left_operators.reshape(split), right_operators, far_left.reshape(split), far_right)
    numbers = jnp.concatenate([sector_rows, *small, *far_small])
    terms = functools.partial(term_products, numbers, near, far, operators, sizes[1])
    got = [send(block, perm=perm) for block, perm in zip(terms(True), FIRST_AXIS)]
    last, own = terms(False)
    got.append(send(last, perm=FIRST_AXIS[2]))
    return regroup(sector_rows, own, got)


def local(
    wavefunction,
    left_operators,
    right_operators,
    source_sector,
    target_sector,
    live_terms,
    sector_rows,
):
    small = (source_sector, target_sector, live_terms)
    branches = [functools.partial(sized, sizes) for sizes in SIZES]
    far_small = tuple(lax.ppermute(numbers, AXES, OTHER_CORE) for numbers in small)
    operands = (wavefunction, left_operators, right_operators, small, far_small, sector_rows)
    keep, *sends = lax.switch(choose(sector_rows, SIZES), branches, *operands)
    got = [lax.ppermute(s, AXES, SECOND_AXIS[k + 1]) for k, s in enumerate(sends)]
    parts = spread(keep, got)
    groups = [[z * 4 + place for z in range(8)] for place in range(4)]
    arrived = lax.all_to_all(
        parts, "term", split_axis=0, concat_axis=0, axis_index_groups=groups, tiled=True
    )
    return finish(sector_rows, arrived)


def solution(mesh):
    in_specs = (
        P("sector", None, None),
        P(("term", "sector"), None, None),
        P(("term", "sector"), None, None),
        P(("term", "sector")),
        P(("term", "sector")),
        P(("term", "sector")),
        P(),
    )
    out_specs = P("sector", "term", None)
    return jax.shard_map(local, mesh=mesh, in_specs=in_specs, out_specs=out_specs, check_vma=False)
```
